256 devices in a mesh: seq: 64 (over y, z, x_hi), samp: 4 (over x_lo, core).
Axes of the slice: x: 4 (x_hi: 2, x_lo: 2; x = x_hi * 2 + x_lo), y: 4, z: 8, core: 2. Of those that a mesh axis runs over, the one named last changes fastest.
Arguments:
- atoms: bfloat16 [48, 32768, 128], P('samp', 'seq'), may hold values from -3 to 3
- gain: float32 [128], replicated, may hold values from 0.25 to 1.75
- w_query: bfloat16 [128, 128], replicated, may hold values from -0.5 to 0.5
- w_key: bfloat16 [128, 128], replicated, may hold values from -0.5 to 0.5
- w_value: bfloat16 [128, 128], replicated, may hold values from -0.5 to 0.5
- w_gate: bfloat16 [128, 128], replicated, may hold values from -0.5 to 0.5
- w_out: bfloat16 [128, 128], replicated, may hold values from -0.5 to 0.5
- w_token: bfloat16 [128, 768], replicated, may hold values from -0.5 to 0.5
- w_pair: bfloat16 [16, 4], replicated, may hold values from -1.5 to 1.5
- pair_cond: bfloat16 [1024, 32, 2048], P('seq'), may hold values from -6 to 6
- counts: int32 [64], replicated, may hold values from 472 to 512, as said below
- membership: int32 [32768], P('seq'), may hold values from 0 to 3071, as said below
- pooled_cot: bfloat16 [48, 3072, 768], P('samp', 'seq'), may hold values from -6 to 6
Outputs:
- pooled: bfloat16 [48, 3072, 768], P('samp', 'seq')
- grad_atoms: bfloat16 [48, 32768, 128], P('samp', 'seq')
- grad_gain: float32 [128], replicated
- grad_query: float32 [128, 128], replicated
- grad_key: float32 [128, 128], replicated
- grad_value: float32 [128, 128], replicated
- grad_gate: float32 [128, 128], replicated
- grad_out: float32 [128, 128], replicated
- grad_token: float32 [128, 768], replicated
- grad_pair: float32 [16, 4], replicated
The draws below stay inside these ranges and needn't reach their ends.
Inputs may be any that keep to these rules, and one draw needn't show every extreme that they name: `counts`: live atoms fill the first slots of each shard; some shard is full. `membership`: slots of shard s name tokens s * 48 to (s + 1) * 48 - 1, never falling along the slots; every token has one or more live atoms; slots past the shard's count name its last token.
All inputs are finite; a program needn't handle non-finite values.
Results may differ from the reference program's by a relative error of at most 0.012.
Values may be sent and summed in bfloat16 or wider, within the bound.
No kernel may reach another device: no remote copies, remote signals or barrier semaphores. Data moves between devices by JAX's collectives and lax.ppermute only.
A program may use at most 128 MiB of HBM per device.

```python
import jax
import jax.numpy as jnp
from jax import lax

D = 128
HEADS = 4
CP = 16
TOKW = 768
QBLK = 32
KWIN = 128
ATOM_DEV = 512
TOK_DEV = 48
ATOMS = 32768
TOKENS = 3072
SAMPLES = 48
N_SEQ = 64


def shard_counts(key):
    base_key = jax.random.fold_in(key, 11)
    drawn_counts = jax.random.randint(jax.random.fold_in(base_key, 1), (N_SEQ,), ATOM_DEV - 40, ATOM_DEV + 1)
    fullest = jax.random.randint(jax.random.fold_in(base_key, 2), (), 0, N_SEQ)
    return jnp.where(jnp.arange(N_SEQ) == fullest, ATOM_DEV, drawn_counts).astype(jnp.int32)


def draw_counts(key, part):
    return shard_counts(key)


def draw_membership(key, part):
    counts = shard_counts(key)
    base_key = jax.random.fold_in(key, 23)
    slot_ids = jnp.arange(ATOM_DEV, dtype=jnp.int32)

    def one_shard(shard_index):
        extra_ids = jax.random.randint(jax.random.fold_in(base_key, shard_index), (ATOM_DEV,), 0, TOK_DEV).astype(jnp.int32)
        values = jnp.where(slot_ids < TOK_DEV, slot_ids, extra_ids)
        values = jnp.where(slot_ids < counts[shard_index], values, TOK_DEV)
        ordered = jnp.minimum(jnp.sort(values), TOK_DEV - 1)
        return ordered + shard_index * TOK_DEV
    return jax.vmap(one_shard)(jnp.arange(N_SEQ, dtype=jnp.int32)).reshape(-1).astype(jnp.int32)


def levels(key, dims, split, smallest, top_value):
    loudness = 1.0
    for axis_at, parts in split:
        steps = jax.random.uniform(jax.random.fold_in(jax.random.fold_in(key, 6), axis_at), (parts,), jnp.float32, smallest / len(split), top_value / len(split))
        loudness = loudness * jnp.repeat(jnp.exp(steps), dims[axis_at] // parts).reshape((-1,) + (1,) * (len(dims) - 1 - axis_at))
    return loudness


def bell_draw(stream_key, shape, scale, limit, cuts=(), held_as=jnp.bfloat16):
    values = jax.random.normal(stream_key, shape, jnp.float32) * scale
    if len(cuts) > 0:
        values = levels(stream_key, shape, cuts, -0.22, 0.18) * values
    return jnp.clip(values, min=-limit, max=limit).astype(held_as)


def setup_inputs(seed: int = 0) -> dict:
    key_list = jax.random.split(jax.random.key(seed), 14)
    atoms = bell_draw(key_list[0], (SAMPLES, ATOMS, D), 0.5, 3.0, ((0, 4), (1, 64)))
    gain = jnp.clip(1.0 + 0.15 * jax.random.normal(key_list[1], (D,), jnp.float32), 0.25, 1.75)
    w_query = bell_draw(key_list[2], (D, D), D ** -0.5, 0.5)
    w_key = bell_draw(key_list[3], (D, D), D ** -0.5, 0.5)
    w_value = bell_draw(key_list[4], (D, D), D ** -0.5, 0.5)
    w_gate = bell_draw(key_list[5], (D, D), D ** -0.5, 0.5)
    w_out = bell_draw(key_list[6], (D, D), D ** -0.5, 0.5)
    w_token = bell_draw(key_list[7], (D, TOKW), D ** -0.5, 0.5)
    w_pair = bell_draw(key_list[8], (CP, HEADS), CP ** -0.5, 1.5)
    pair_cond = bell_draw(key_list[9], (ATOMS // QBLK, QBLK, KWIN * CP), 1.0, 6.0, ((0, 64),))
    counts = draw_counts(jax.random.fold_in(key_list[13], 71), 0)
    membership = draw_membership(jax.random.fold_in(key_list[13], 71), 0)
    pooled_cot = bell_draw(key_list[12], (SAMPLES, TOKENS, TOKW), 1.0, 6.0, ((0, 4), (1, 64)))
    return {"atoms": atoms, "gain": gain, "w_query": w_query, "w_key": w_key, "w_value": w_value, "w_gate": w_gate, "w_out": w_out, "w_token": w_token, "w_pair": w_pair, "pair_cond": pair_cond, "counts": counts, "membership": membership, "pooled_cot": pooled_cot}


epsilon = 1e-05
highest = lax.Precision.HIGHEST

def windows(extended, blocks):
    span_blocks = KWIN // QBLK
    blocked = extended.reshape((blocks + span_blocks - 1, QBLK) + extended.shape[1:])
    return jnp.concatenate([blocked[offset:offset + blocks] for offset in range(span_blocks)], axis=1)

def unwindow(grad_windows, blocks):
    span_blocks = KWIN // QBLK
    summed = None
    for offset in range(span_blocks):
        grad_piece = grad_windows[:, offset * QBLK:(offset + 1) * QBLK]
        pad_widths = [(offset, span_blocks - 1 - offset)] + [(0, 0)] * (grad_piece.ndim - 1)
        padded = jnp.pad(grad_piece, pad_widths)
        summed = padded if summed is None else summed + padded
    return summed.reshape((QBLK * (blocks + span_blocks - 1),) + grad_windows.shape[2:])

def rounded(value):
    return lax.optimization_barrier(value.astype(jnp.bfloat16)).astype(jnp.float32)

def sample_pass(atoms, queries, keys_ext, values_ext, gate_pre, key_mask, pair_bias, w_out, w_token, member, inv_count, cotangent):
    atom_rows, model_width = atoms.shape
    blocks = atom_rows // QBLK
    head_dim = model_width // HEADS
    scaling = head_dim ** (-0.5)
    query_heads = queries.reshape(blocks, QBLK, HEADS, head_dim).astype(jnp.float32)
    key_heads = windows(keys_ext, blocks).reshape(blocks, KWIN, HEADS, head_dim).astype(jnp.float32)
    value_heads = windows(values_ext, blocks).reshape(blocks, KWIN, HEADS, head_dim).astype(jnp.float32)
    scores = jnp.einsum('bihd,bjhd->bhij', query_heads, key_heads) * scaling + pair_bias
    exp_scores = jnp.where(key_mask[:, None, None, :], jnp.exp(scores), 0.0)
    attn_probs = exp_scores / lax.optimization_barrier(jnp.sum(exp_scores, axis=-1, keepdims=True))
    probs_low = rounded(attn_probs)
    attended = jnp.einsum('bhij,bjhd->bihd', probs_low, value_heads).reshape(atom_rows, model_width)
    gate_sig = jax.nn.sigmoid(gate_pre)
    gated_out = (gate_sig * attended).astype(jnp.bfloat16)
    updated = (atoms.astype(jnp.float32) + jnp.dot(gated_out, w_out, preferred_element_type=jnp.float32)).astype(jnp.bfloat16)
    token_pre = jnp.dot(updated, w_token, preferred_element_type=jnp.float32)
    token_sig = jax.nn.sigmoid(token_pre)
    token_act = (token_pre * token_sig).astype(jnp.bfloat16)
    shards = member.shape[0]
    channels = token_act.shape[-1]
    grouped = token_act.reshape(shards, -1, channels).astype(jnp.float32)
    member_f = member.astype(jnp.float32)
    pooled = (jnp.einsum('sat,sac->stc', member_f, grouped) * inv_count[:, :, None]).astype(jnp.bfloat16)
    pooled = pooled.reshape(-1, channels)
    scaled_cot = cotangent.reshape(shards, -1, channels).astype(jnp.float32) * inv_count[:, :, None]
    grad_act = jnp.einsum('sat,stc->sac', member_f, scaled_cot, precision=highest).reshape(atom_rows, channels)
    grad_pre = (grad_act * token_sig * (1.0 + token_pre * (1.0 - token_sig))).astype(jnp.bfloat16)
    grad_token = jnp.dot(updated.T, grad_pre, preferred_element_type=jnp.float32)
    grad_updated = jnp.dot(grad_pre, w_token.T, preferred_element_type=jnp.float32).astype(jnp.bfloat16)
    grad_outw = jnp.dot(gated_out.T, grad_updated, preferred_element_type=jnp.float32)
    grad_gated = jnp.dot(grad_updated, w_out.T, preferred_element_type=jnp.float32)
    grad_gatepre = (grad_gated * attended * gate_sig * (1.0 - gate_sig)).astype(jnp.bfloat16)
    grad_att = rounded(grad_gated * gate_sig)
    grad_heads = grad_att.reshape(blocks, QBLK, HEADS, head_dim)
    grad_probs = jnp.einsum('bihd,bjhd->bhij', grad_heads, value_heads)
    grad_scores = attn_probs * (grad_probs - lax.optimization_barrier(jnp.sum(attn_probs * grad_probs, axis=-1, keepdims=True)))
    scores_low = rounded(grad_scores)
    grad_queries = jnp.einsum('bhij,bjhd->bihd', scores_low, key_heads).reshape(atom_rows, model_width) * scaling
    grad_key_win = jnp.einsum('bhij,bihd->bjhd', scores_low, query_heads).reshape(blocks, KWIN, model_width) * scaling
    grad_value_win = jnp.einsum('bhij,bihd->bjhd', probs_low, grad_heads).reshape(blocks, KWIN, model_width)
    return (pooled, grad_updated, grad_queries, unwindow(grad_key_win, blocks), unwindow(grad_value_win, blocks), grad_gatepre, grad_outw, grad_token, grad_scores)

def reference(atoms, gain, w_query, w_key, w_value, w_gate, w_out, w_token, w_pair, pair_cond, counts, membership, pooled_cot):
    rim_width = (KWIN - QBLK) // 2
    blocks = ATOMS // QBLK
    slot_ids = jnp.arange(ATOMS, dtype=jnp.int32)
    alive_slots = slot_ids % ATOM_DEV < counts[slot_ids // ATOM_DEV]
    key_mask = windows(jnp.pad(alive_slots, (rim_width, rim_width)), blocks)
    pair_f = pair_cond.reshape(blocks, QBLK, KWIN, CP).astype(jnp.float32)
    pair_bias = jnp.einsum('bijc,ch->bhij', pair_f, w_pair.astype(jnp.float32))
    local_ids = membership.reshape(N_SEQ, ATOM_DEV) - (jnp.arange(N_SEQ, dtype=jnp.int32) * TOK_DEV)[:, None]
    member = ((local_ids[:, :, None] == jnp.arange(TOK_DEV, dtype=jnp.int32)[None, None, :]) & alive_slots.reshape(N_SEQ, ATOM_DEV)[:, :, None]).astype(jnp.bfloat16)
    inv_count = 1.0 / lax.optimization_barrier(jnp.sum(member.astype(jnp.float32), axis=1))

    def per_sample(totals, inputs):
        sample_atoms, cotangent = inputs
        atoms_f = sample_atoms.astype(jnp.float32)
        centred = atoms_f - lax.optimization_barrier(jnp.mean(atoms_f, axis=-1, keepdims=True))
        variance = lax.optimization_barrier(jnp.mean(centred * centred, axis=-1, keepdims=True))
        inv_std = lax.rsqrt(variance + epsilon)
        normed = centred * inv_std
        hidden = (normed * gain).astype(jnp.bfloat16)
        queries = jnp.dot(hidden, w_query, preferred_element_type=jnp.float32).astype(jnp.bfloat16)
        keys = jnp.dot(hidden, w_key, preferred_element_type=jnp.float32).astype(jnp.bfloat16)
        values = jnp.dot(hidden, w_value, preferred_element_type=jnp.float32).astype(jnp.bfloat16)
        gate_pre = jnp.dot(hidden, w_gate, preferred_element_type=jnp.float32)
        keys_ext = jnp.pad(keys, ((rim_width, rim_width), (0, 0)))
        values_ext = jnp.pad(values, ((rim_width, rim_width), (0, 0)))
        pooled, grad_updated, grad_queries, grad_keys_ext, grad_values_ext, grad_gatepre, grad_outw, grad_tokw, grad_scores = sample_pass(sample_atoms, queries, keys_ext, values_ext, gate_pre, key_mask, pair_bias, w_out, w_token, member, inv_count, cotangent)
        grad_q_low = grad_queries.astype(jnp.bfloat16)
        grad_k_low = grad_keys_ext[rim_width:rim_width + ATOMS].astype(jnp.bfloat16)
        grad_v_low = grad_values_ext[rim_width:rim_width + ATOMS].astype(jnp.bfloat16)
        grad_hidden = jnp.dot(grad_q_low, w_query.T, preferred_element_type=jnp.float32) + jnp.dot(grad_k_low, w_key.T, preferred_element_type=jnp.float32) + jnp.dot(grad_v_low, w_value.T, preferred_element_type=jnp.float32) + jnp.dot(grad_gatepre, w_gate.T, preferred_element_type=jnp.float32)
        grad_normed = grad_hidden * gain
        grad_ln = inv_std * (grad_normed - lax.optimization_barrier(jnp.mean(grad_normed, axis=-1, keepdims=True)) - normed * lax.optimization_barrier(jnp.mean(grad_normed * normed, axis=-1, keepdims=True)))
        grad_sample = (grad_updated.astype(jnp.float32) + grad_ln).astype(jnp.bfloat16)
        acc_gain, acc_query, acc_key, acc_value, acc_gate, acc_out, acc_token, acc_scores = totals
        totals = (acc_gain + lax.optimization_barrier(jnp.sum(grad_hidden * normed, axis=0)), acc_query + jnp.dot(hidden.T, grad_q_low, preferred_element_type=jnp.float32), acc_key + jnp.dot(hidden.T, grad_k_low, preferred_element_type=jnp.float32), acc_value + jnp.dot(hidden.T, grad_v_low, preferred_element_type=jnp.float32), acc_gate + jnp.dot(hidden.T, grad_gatepre, preferred_element_type=jnp.float32), acc_out + grad_outw, acc_token + grad_tokw, acc_scores + grad_scores)
        return (totals, (pooled, grad_sample))
    start = (jnp.zeros((D,), jnp.float32), jnp.zeros((D, D), jnp.float32), jnp.zeros((D, D), jnp.float32), jnp.zeros((D, D), jnp.float32), jnp.zeros((D, D), jnp.float32), jnp.zeros((D, D), jnp.float32), jnp.zeros((D, TOKW), jnp.float32), jnp.zeros((blocks, HEADS, QBLK, KWIN), jnp.float32))
    totals, (pooled, grad_atoms) = lax.scan(per_sample, start, (atoms, pooled_cot))
    grad_gain, grad_query, grad_key, grad_value, grad_gate, grad_out, grad_token, score_sum = totals
    grad_pair = jnp.einsum('bijc,bhij->ch', pair_f, score_sum)
    return (pooled, grad_atoms, grad_gain, grad_query, grad_key, grad_value, grad_gate, grad_out, grad_token, grad_pair)
```

```python
import jax
import jax.numpy as jnp
from jax import lax
from jax.experimental import pallas as pl
from jax.experimental.pallas import tpu as pltpu
from jax.sharding import PartitionSpec as P

HEADS = 4
QBLK = 32
KWIN = 128
TOK_DEV = 48
RIM = (KWIN - QBLK) // 2
D = 128
CP = 16

epsilon = 1e-05
LOG2E = 1.4426950408889634
LN2 = 0.6931471805599453
SCALING = 32.0 ** -0.5
F32 = jnp.float32
BF16 = jnp.bfloat16
VMEM_LIMIT = 56 * 1024 * 1024


def dot(a, b):
    return lax.dot_general(a, b, (((1,), (0,)), ((), ())), preferred_element_type=F32)


def dot_t(a, b):
    return lax.dot_general(a, b, (((1,), (1,)), ((), ())), preferred_element_type=F32)


def t_dot(a, b):
    return lax.dot_general(a, b, (((0,), (0,)), ((), ())), preferred_element_type=F32)


def iota(shape, dim):
    return lax.broadcasted_iota(jnp.int32, shape, dim)


def bias_kernel(meta_ref, pair_ref, wcol_ref, bias_ref, w_scr):
    rows = pair_ref.shape[0]
    span = w_scr.shape[1]
    key_of_row = iota((KWIN, CP, span), 0)
    key_of_lane = iota((KWIN, CP, span), 2) % KWIN
    wide = jnp.broadcast_to(wcol_ref[...][None], (KWIN, CP, span))
    w_scr[...] = (
        jnp.where(key_of_row == key_of_lane, wide, 0.0).astype(BF16).reshape(KWIN * CP, span)
    )
    atom_rows = rows
    left, own, right = meta_ref[0], meta_ref[1], meta_ref[2]
    step = 128
    for r0 in range(0, rows, step):
        out = dot(pair_ref[r0 : r0 + step, :], w_scr[...])
        for q0 in range(0, step, QBLK):
            b = (r0 + q0) // QBLK
            slot = iota((1, KWIN), 1) + (b * QBLK - RIM)
            before, after = slot < 0, slot >= atom_rows
            limit = jnp.where(before, left, jnp.where(after, right, own))
            place = jnp.where(
                before, slot + atom_rows, jnp.where(after, slot - atom_rows, slot)
            )
            shift = jnp.where(place < limit, 0.0, -jnp.inf)
            for h in range(HEADS):
                bias_ref[b, h * QBLK : (h + 1) * QBLK, :] = (
                    out[q0 : q0 + QBLK, h * KWIN : (h + 1) * KWIN] * LOG2E + shift
                )


def pair_bias_call(meta, pair, wcol):
    blocks = pair.shape[0] // QBLK
    return pl.pallas_call(
        bias_kernel,
        out_shape=jax.ShapeDtypeStruct((blocks, HEADS * QBLK, KWIN), F32),
        in_specs=[
            pl.BlockSpec(memory_space=pltpu.SMEM),
            pl.BlockSpec(memory_space=pltpu.VMEM),
            pl.BlockSpec(memory_space=pltpu.VMEM),
        ],
        out_specs=pl.BlockSpec(memory_space=pltpu.VMEM),
        scratch_shapes=[pltpu.VMEM((KWIN * CP, HEADS * KWIN), BF16)],
        compiler_params=pltpu.CompilerParams(vmem_limit_bytes=VMEM_LIMIT),
        cost_estimate=pl.CostEstimate(
            flops=2 * pair.shape[0] * KWIN * CP * HEADS * KWIN,
            bytes_accessed=5 << 20,
            transcendentals=0,
        ),
        name="pair_bias",
    )(meta, pair, wcol)


def pair_grad_kernel(pair_ref, score_ref, out_ref, g_scr):
    blocks = score_ref.shape[0]
    wide = KWIN * CP
    key_of_lane = iota((KWIN, wide), 1) // CP
    own_key = key_of_lane == iota((KWIN, wide), 0)
    rows = []
    for h in range(HEADS):
        for b in range(blocks):
            g_scr[b * QBLK : (b + 1) * QBLK, :] = score_ref[
                b, h * QBLK : (h + 1) * QBLK, :
            ].astype(BF16)
        prod = t_dot(g_scr[...], pair_ref[...])
        rows.append(jnp.sum(jnp.where(own_key, prod, 0.0), axis=0, keepdims=True))
    stacked = jnp.concatenate(rows + [jnp.zeros((8 - HEADS, wide), F32)], axis=0)
    out_ref[...] = stacked


def pair_grad_call(pair, score_sum):
    return pl.pallas_call(
        pair_grad_kernel,
        out_shape=jax.ShapeDtypeStruct((8, KWIN * CP), F32),
        in_specs=[pl.BlockSpec(memory_space=pltpu.VMEM)] * 2,
        out_specs=pl.BlockSpec(memory_space=pltpu.VMEM),
        scratch_shapes=[pltpu.VMEM((pair.shape[0], KWIN), BF16)],
        compiler_params=pltpu.CompilerParams(vmem_limit_bytes=VMEM_LIMIT),
        cost_estimate=pl.CostEstimate(
            flops=2 * pair.shape[0] * KWIN * CP * HEADS * KWIN,
            bytes_accessed=3 << 20,
            transcendentals=0,
        ),
        name="pair_grad",
    )(pair, score_sum)


def layer_norm(x):
    mean = jnp.mean(x, axis=-1, keepdims=True)
    centred = x - mean
    variance = jnp.mean(centred * centred, axis=-1, keepdims=True)
    inv_std = lax.rsqrt(variance + epsilon)
    return centred * inv_std, inv_std


def ln_backward(gh, gain, normed, inv_std):
    gn = gh * gain
    return inv_std * (
        gn
        - jnp.mean(gn, axis=-1, keepdims=True)
        - normed * jnp.mean(gn * normed, axis=-1, keepdims=True)
    )


def pick_heads(o):
    head = iota((QBLK, D), 1) // (D // HEADS)
    r = o[0:QBLK]
    for h in range(1, HEADS):
        r = jnp.where(head == h, o[h * QBLK : (h + 1) * QBLK], r)
    return r


def main_kernel(
    meta_ref,
    memb_ref,
    atoms_ref,
    low_ref,
    high_ref,
    cot_ref,
    gain_ref,
    wqg_ref,
    wkv_ref,
    wcat_ref,
    wout_ref,
    wtok_ref,
    bias_ref,
    pooled_ref,
    gatoms_ref,
    rim_ref,
    send_ref,
    accw_ref,
    accout_ref,
    acctok_ref,
    gain_acc_ref,
    score_ref,
    mem_t,
    mem2,
    inv_scr,
    hid,
    nrm,
    k_ext,
    v1,
    q_scr,
    sig_scr,
    att_scr,
    rden_scr,
    q4_scr,
    e_scr,
    upd_scr,
    act_scr,
    gpre_scr,
    g_scr,
    nga_scr,
    gk_ext,
    gv_ext,
    gcat,
    gu_scr,
):
    rows = atoms_ref.shape[1]
    ext = rows + 2 * RIM
    blocks = rows // QBLK
    step = pl.program_id(0)
    mask4 = (
        (iota((HEADS * QBLK, D), 0) // QBLK == iota((HEADS * QBLK, D), 1) // (D // HEADS))
        .astype(F32)
        .astype(BF16)
    )

    @pl.when(step == 0)
    def _():
        accw_ref[...] = jnp.zeros_like(accw_ref)
        accout_ref[...] = jnp.zeros_like(accout_ref)
        acctok_ref[...] = jnp.zeros_like(acctok_ref)
        gain_acc_ref[...] = jnp.zeros_like(gain_acc_ref)
        score_ref[...] = jnp.zeros_like(score_ref)
        v1[:, D:] = jnp.ones((ext, D), BF16)
        own, first = meta_ref[1], meta_ref[3]
        local = memb_ref[...] - first
        slot = iota((D, rows), 1)
        hit = (local == iota((D, rows), 0)) & (slot < own)
        hit_f = jnp.where(hit, 1.0, 0.0)
        total = jnp.sum(hit_f, axis=1, keepdims=True)
        inv = 1.0 / jnp.maximum(total, 1.0)
        mem_t[...] = hit_f[0:TOK_DEV].astype(BF16)
        inv_scr[...] = jnp.broadcast_to(inv[0:TOK_DEV], inv_scr.shape)
        weighted = hit_f * inv
        high = weighted.astype(BF16)
        rest = (weighted - high.astype(F32)).astype(BF16)
        mem2[:, 0:TOK_DEV] = high.astype(F32).T.astype(BF16)[:, 0:TOK_DEV]
        mem2[:, TOK_DEV : 2 * TOK_DEV] = rest.astype(F32).T.astype(BF16)[:, 0:TOK_DEV]

    gain = gain_ref[...]
    for name, r0, n in (("low", 0, RIM), ("own", RIM, rows), ("high", RIM + rows, RIM)):
        src = {"low": low_ref, "own": atoms_ref, "high": high_ref}[name]
        size = n if n < 128 else 128
        for c0 in range(0, n, size):
            x = src[0, c0 : c0 + size, :].astype(F32)
            normed, inv_std = layer_norm(x)
            hidden = (normed * gain).astype(BF16)
            kv = dot(hidden, wkv_ref[...]).astype(BF16)
            k_ext[r0 + c0 : r0 + c0 + size, :] = kv[:, 0:D]
            v1[r0 + c0 : r0 + c0 + size, 0:D] = kv[:, D:]
            if name == "own":
                hid[c0 : c0 + size, :] = hidden
                nrm[c0 : c0 + size, :] = normed
                qg = dot(hidden, wqg_ref[...])
                q_scr[c0 : c0 + size, :] = (qg[:, 0:D] * (SCALING * LOG2E)).astype(BF16)
                sig_scr[c0 : c0 + size, :] = 0.5 * jnp.tanh(0.5 * qg[:, D:]) + 0.5

    for b in range(blocks):
        r0 = b * QBLK
        q_b = q_scr[r0 : r0 + QBLK, :]
        q4 = jnp.concatenate([q_b] * HEADS, axis=0) * mask4
        q4_scr[b] = q4
        scores = dot_t(q4, k_ext[r0 : r0 + KWIN, :]) + bias_ref[b]
        e = jnp.exp2(scores).astype(BF16)
        e_scr[b] = e
        o = dot(e, v1[r0 : r0 + KWIN, :])
        num = pick_heads(o[:, 0:D])
        rden = 1.0 / pick_heads(o[:, D:])
        att_scr[r0 : r0 + QBLK, :] = num * rden
        rden_scr[r0 : r0 + QBLK, :] = rden

    cot = cot_ref[0]
    cot2 = jnp.concatenate([cot, cot], axis=0)
    size = 128
    cols = 256
    width = wtok_ref.shape[1]
    for c0 in range(0, rows, size):
        sl = slice(c0, c0 + size)
        gated = (sig_scr[sl, :] * att_scr[sl, :]).astype(BF16)
        upd = (atoms_ref[0, sl, :].astype(F32) + dot(gated, wout_ref[...])).astype(BF16)
        upd_scr[sl, :] = upd
        for t0 in range(0, width, cols):
            cs = slice(t0, t0 + cols)
            pre = dot(upd, wtok_ref[:, cs])
            sg = 0.5 * jnp.tanh(0.5 * pre) + 0.5
            act = pre * sg
            act_scr[sl, cs] = act.astype(BF16)
            grad_act = dot(mem2[sl, :], cot2[:, cs])
            gpre_scr[sl, cs] = (grad_act * (sg + act * (1.0 - sg))).astype(BF16)
    for t0 in range(0, width, cols):
        cs = slice(t0, t0 + cols)
        pooled_ref[0, :, cs] = (
            dot(mem_t[...], act_scr[:, cs]) * jnp.concatenate([inv_scr[...]] * (cols // D), axis=1)
        ).astype(BF16)
        acctok_ref[:, cs] += t_dot(upd_scr[...], gpre_scr[:, cs])
    for c0 in range(0, rows, size):
        sl = slice(c0, c0 + size)
        gu = dot_t(gpre_scr[sl, :], wtok_ref[...]).astype(BF16)
        gu_scr[sl, :] = gu
        sig = sig_scr[sl, :]
        att = att_scr[sl, :]
        gated = (sig * att).astype(BF16)
        accout_ref[...] += t_dot(gated, gu)
        gatt = dot_t(gu, wout_ref[...]) * sig
        gatt_att = gatt * att
        gcat[sl, 3 * D :] = (gatt_att * (1.0 - sig)).astype(BF16)
        rden = rden_scr[sl, :]
        g_scr[sl, :] = (gatt * rden).astype(BF16)
        nga_scr[sl, :] = (-(gatt_att * rden)).astype(BF16)

    gk_ext[...] = jnp.zeros_like(gk_ext)
    gv_ext[...] = jnp.zeros_like(gv_ext)
    for b in range(blocks):
        r0 = b * QBLK
        g4 = jnp.concatenate([g_scr[r0 : r0 + QBLK, :]] * HEADS, axis=0) * mask4
        nga4 = jnp.concatenate([nga_scr[r0 : r0 + QBLK, :]] * HEADS, axis=0) * mask4
        e = e_scr[b]
        dp = dot_t(jnp.concatenate([g4, nga4], axis=1), v1[r0 : r0 + KWIN, :])
        ds = e.astype(F32) * dp
        score_ref[b] += ds
        dsl = ds.astype(BF16)
        gq = pick_heads(dot(dsl, k_ext[r0 : r0 + KWIN, :]))
        gcat[r0 : r0 + QBLK, 0:D] = (gq * SCALING).astype(BF16)
        gk_ext[r0 : r0 + KWIN, :] += t_dot(dsl, q4_scr[b])
        gv_ext[r0 : r0 + KWIN, :] += t_dot(e, g4)

    send_ref[0, 0, 0] = (gk_ext[0:RIM, :] * LN2).astype(BF16)
    send_ref[0, 0, 1] = gv_ext[0:RIM, :].astype(BF16)
    send_ref[0, 1, 0] = (gk_ext[RIM + rows :, :] * LN2).astype(BF16)
    send_ref[0, 1, 1] = gv_ext[RIM + rows :, :].astype(BF16)

    for c0 in range(0, rows, size):
        sl = slice(c0, c0 + size)
        es = slice(c0 + RIM, c0 + RIM + size)
        gcat[sl, D : 2 * D] = (gk_ext[es, :] * LN2).astype(BF16)
        gcat[sl, 2 * D : 3 * D] = gv_ext[es, :].astype(BF16)
        gh = dot_t(gcat[sl, :], wcat_ref[...])
        normed = nrm[sl, :]
        gain_acc_ref[...] += jnp.sum((gh * normed).reshape(size // 8, 8, D), axis=0)
        x = atoms_ref[0, sl, :].astype(F32)
        centred = x - jnp.mean(x, axis=-1, keepdims=True)
        inv_std = lax.rsqrt(jnp.mean(centred * centred, axis=-1, keepdims=True) + epsilon)
        ga = gu_scr[sl, :].astype(F32) + ln_backward(gh, gain, normed, inv_std)
        gatoms_ref[0, sl, :] = ga.astype(BF16)
        if c0 == 0:
            rim_ref[0, 0:RIM, :] = ga[0:RIM]
        if c0 + size == rows:
            rim_ref[0, RIM:, :] = ga[size - RIM :]
    accw_ref[...] += t_dot(hid[...], gcat[...])


def main_call(meta, memb, atoms, low, high, cot, gain, wqg, wkv, wcat, wout, wtok, bias):
    samples, rows, _ = atoms.shape
    ext = rows + 2 * RIM
    width = wtok.shape[1]
    blocks = rows // QBLK
    hq = HEADS * QBLK

    def per_sample(*shape):
        return pl.BlockSpec((1,) + shape, lambda s: (s,) + (0,) * len(shape))

    def whole(*shape):
        return pl.BlockSpec(shape, lambda s: (0,) * len(shape))

    sd = jax.ShapeDtypeStruct
    return pl.pallas_call(
        main_kernel,
        grid=(samples,),
        out_shape=(
            sd((samples, TOK_DEV, width), BF16),
            sd((samples, rows, D), BF16),
            sd((samples, 2 * RIM, D), F32),
            sd((samples, 2, 2, RIM, D), BF16),
            sd((D, 4 * D), F32),
            sd((D, D), F32),
            sd((D, width), F32),
            sd((8, D), F32),
            sd((blocks, hq, KWIN), F32),
        ),
        in_specs=[
            pl.BlockSpec(memory_space=pltpu.SMEM),
            whole(1, rows),
            per_sample(rows, D),
            per_sample(RIM, D),
            per_sample(RIM, D),
            per_sample(TOK_DEV, width),
            whole(1, D),
            whole(D, 2 * D),
            whole(D, 2 * D),
            whole(D, 4 * D),
            whole(D, D),
            whole(D, width),
            whole(blocks, hq, KWIN),
        ],
        out_specs=(
            per_sample(TOK_DEV, width),
            per_sample(rows, D),
            per_sample(2 * RIM, D),
            per_sample(2, 2, RIM, D),
            whole(D, 4 * D),
            whole(D, D),
            whole(D, width),
            whole(8, D),
            whole(blocks, hq, KWIN),
        ),
        scratch_shapes=[
            pltpu.VMEM((TOK_DEV, rows), BF16),
            pltpu.VMEM((rows, 2 * TOK_DEV), BF16),
            pltpu.VMEM((TOK_DEV, D), F32),
            pltpu.VMEM((rows, D), BF16),
            pltpu.VMEM((rows, D), F32),
            pltpu.VMEM((ext, D), BF16),
            pltpu.VMEM((ext, 2 * D), BF16),
            pltpu.VMEM((rows, D), BF16),
            pltpu.VMEM((rows, D), F32),
            pltpu.VMEM((rows, D), F32),
            pltpu.VMEM((rows, D), F32),
            pltpu.VMEM((blocks, hq, D), BF16),
            pltpu.VMEM((blocks, hq, KWIN), BF16),
            pltpu.VMEM((rows, D), BF16),
            pltpu.VMEM((rows, width), BF16),
            pltpu.VMEM((rows, width), BF16),
            pltpu.VMEM((rows, D), BF16),
            pltpu.VMEM((rows, D), BF16),
            pltpu.VMEM((ext, D), F32),
            pltpu.VMEM((ext, D), F32),
            pltpu.VMEM((rows, 4 * D), BF16),
            pltpu.VMEM((rows, D), BF16),
        ],
        compiler_params=pltpu.CompilerParams(
            vmem_limit_bytes=VMEM_LIMIT, dimension_semantics=("arbitrary",)
        ),
        name="atom_layer",
    )(meta, memb, atoms, low, high, cot, gain, wqg, wkv, wcat, wout, wtok, bias)


def rim_kernel(
    atoms_ref, part_ref, recv_ref, gain_ref, wkv_ref, _, gatoms_ref, wk_ref, gacc_ref
):
    step = pl.program_id(0)
    samples, size, _w = atoms_ref.shape

    @pl.when(step == 0)
    def _():
        wk_ref[...] = jnp.zeros_like(wk_ref)
        gacc_ref[...] = jnp.zeros_like(gacc_ref)

    flat = samples * size
    x = atoms_ref[...].reshape(flat, D).astype(F32)
    normed, inv_std = layer_norm(x)
    gain = gain_ref[...]
    hidden = (normed * gain).astype(BF16)
    gkv = jnp.concatenate(
        [recv_ref[:, 0].reshape(flat, D), recv_ref[:, 1].reshape(flat, D)], axis=1
    )
    gh = dot_t(gkv, wkv_ref[...])
    wk_ref[...] += t_dot(hidden, gkv)
    gacc_ref[...] += jnp.sum((gh * normed).reshape(flat // 8, 8, D), axis=0)
    ga = part_ref[...].reshape(flat, D) + ln_backward(gh, gain, normed, inv_std)
    gatoms_ref[...] = ga.astype(BF16).reshape(samples, size, D)


def rim_call(atoms, part, recv, gain, wkv, gatoms):
    samples, rows, _ = atoms.shape
    size = 16
    half = RIM // size
    skip = rows // size - 2 * half

    def edge(i):
        return jnp.where(i < half, i, i + skip)

    return pl.pallas_call(
        rim_kernel,
        grid=(2 * half,),
        out_shape=(
            jax.ShapeDtypeStruct(gatoms.shape, BF16),
            jax.ShapeDtypeStruct((D, 2 * D), F32),
            jax.ShapeDtypeStruct((8, D), F32),
        ),
        in_specs=[
            pl.BlockSpec((samples, size, D), lambda i: (0, edge(i), 0)),
            pl.BlockSpec((samples, size, D), lambda i: (0, i, 0)),
            pl.BlockSpec((samples, 2, size, D), lambda i: (0, 0, i, 0)),
            pl.BlockSpec((1, D), lambda i: (0, 0)),
            pl.BlockSpec((D, 2 * D), lambda i: (0, 0)),
            pl.BlockSpec(memory_space=pl.ANY),
        ],
        out_specs=(
            pl.BlockSpec((samples, size, D), lambda i: (0, edge(i), 0)),
            pl.BlockSpec((D, 2 * D), lambda i: (0, 0)),
            pl.BlockSpec((8, D), lambda i: (0, 0)),
        ),
        input_output_aliases={5: 0},
        compiler_params=pltpu.CompilerParams(dimension_semantics=("arbitrary",)),
        name="rim_rows",
    )(atoms, part, recv, gain, wkv, gatoms)


def digits_of(axis, strides):
    return axis, strides


def route(count, digits, k):
    out = []
    total = 1
    for _, size in digits:
        total *= size
    for i in range(count):
        c, m = 0, 1
        for stride, size in digits:
            c += (i // stride % size) * m
            m *= size
        q = (c + k) % total
        j = i
        for stride, size in digits:
            j += (q % size - i // stride % size) * stride
            q //= size
        out.append((i, j))
    return out


def group_size(digits):
    total = 1
    for _, size in digits:
        total *= size
    return total


def exchange_sum(x, axis, digits):
    count = lax.axis_size(axis)
    low = x.astype(BF16)
    total = low.astype(F32)
    for k in range(1, group_size(digits)):
        total = total + lax.ppermute(low, axis, route(count, digits, k)).astype(F32)
    return total


def scatter_sum(x, axis):
    count = lax.axis_size(axis)
    me = lax.axis_index(axis)
    size = x.shape[0] // count
    low = x.astype(BF16)
    total = lax.dynamic_slice_in_dim(x, me * size, size, 0)
    for k in range(1, count):
        piece = lax.dynamic_slice_in_dim(low, (me + k) % count * size, size, 0)
        total = total + lax.ppermute(piece, axis, route(count, [(1, count)], k)).astype(F32)
    return total


def gather(x, axis):
    count = lax.axis_size(axis)
    me = lax.axis_index(axis)
    size = x.shape[0]
    low = x.astype(BF16)
    out = jnp.zeros((count * size,) + x.shape[1:], BF16)
    out = lax.dynamic_update_slice_in_dim(out, low, me * size, 0)
    for k in range(1, count):
        piece = lax.ppermute(low, axis, route(count, [(1, count)], k))
        out = lax.dynamic_update_slice_in_dim(out, piece, (me - k) % count * size, 0)
    return out


def seq_stages(count):
    stages, stride = [], 1
    while stride < count:
        size = min(4, count // stride)
        stages.append([(stride, size)])
        stride *= size
    return stages


def sum_everywhere(x):
    x = scatter_sum(x, "samp")
    for digits in seq_stages(lax.axis_size("seq")):
        x = exchange_sum(x, "seq", digits)
    return gather(x, "samp").astype(F32)


def shifted(block, axis, distance):
    devices = range(lax.axis_size(axis))
    moves = [(i - distance, i) for i in devices if i - distance in devices]
    return lax.ppermute(block, axis, moves)


def on_device(
    atoms,
    gain,
    w_query,
    w_key,
    w_value,
    w_gate,
    w_out,
    w_token,
    w_pair,
    pair_cond,
    counts,
    membership,
    pooled_cot,
):
    seq_count = lax.axis_size("seq")
    shard = lax.axis_index("seq")
    samples, rows, _ = atoms.shape
    low = shifted(atoms[:, rows - RIM :], "seq", 1)
    high = shifted(atoms[:, :RIM], "seq", -1)
    left_count = jnp.where(shard > 0, counts[jnp.maximum(shard - 1, 0)], 0)
    right_count = jnp.where(
        shard < seq_count - 1, counts[jnp.minimum(shard + 1, seq_count - 1)], 0
    )
    meta = jnp.stack([left_count, counts[shard], right_count, shard * TOK_DEV]).astype(jnp.int32)
    pair = pair_cond.reshape(rows, KWIN * CP)
    wcol = jnp.repeat(w_pair.astype(F32), KWIN, axis=1)
    bias = pair_bias_call(meta, pair, wcol)
    gain_row = gain.reshape(1, D)
    wqg = jnp.concatenate([w_query, w_gate], axis=1)
    wkv = jnp.concatenate([w_key, w_value], axis=1)
    wcat = jnp.concatenate([w_query, w_key, w_value, w_gate], axis=1)
    pooled, gatoms, rim_part, send, accw, acc_out, acc_tok, gain_acc, score_sum = main_call(
        meta,
        membership.reshape(1, rows),
        atoms,
        low,
        high,
        pooled_cot,
        gain_row,
        wqg,
        wkv,
        wcat,
        w_out,
        w_token,
        bias,
    )
    from_right = shifted(send[:, 0], "seq", -1)
    from_left = shifted(send[:, 1], "seq", 1)
    pair_part = pair_grad_call(pair, score_sum)
    recv = jnp.concatenate([from_left, from_right], axis=2)
    grad_atoms, rim_w, rim_gain = rim_call(atoms, rim_part, recv, gain_row, wkv, gatoms)
    pair_sum = jnp.sum(pair_part[:HEADS].reshape(HEADS, KWIN, CP), axis=1).reshape(1, HEADS * CP)
    gain_sum = jnp.sum(gain_acc + rim_gain, axis=0, keepdims=True)
    small = jnp.concatenate(
        [
            gain_sum,
            jnp.pad(pair_sum, ((0, 0), (0, D - HEADS * CP))),
        ],
        axis=0,
    )
    width = w_token.shape[1]
    pieces = [
        accw[:, 0:D],
        accw[:, D : 2 * D] + rim_w[:, 0:D],
        accw[:, 2 * D : 3 * D] + rim_w[:, D:],
        accw[:, 3 * D :],
        acc_out,
    ] + [acc_tok[:, c : c + D] for c in range(0, width, D)]
    pieces.append(jnp.pad(small, ((0, 64 - small.shape[0]), (0, 0))))
    flat = sum_everywhere(jnp.concatenate(pieces, axis=0))
    mats = [flat[i * D : (i + 1) * D] for i in range(5 + width // D)]
    tail = flat[(5 + width // D) * D :]
    grad_pair = tail[1, : HEADS * CP].reshape(HEADS, CP).T
    return (
        pooled,
        grad_atoms,
        tail[0],
        mats[0],
        mats[1],
        mats[2],
        mats[3],
        mats[4],
        jnp.concatenate(mats[5:], axis=1),
        grad_pair,
    )


def solution(mesh):
    placed = (
        P("samp", "seq", None),
        P(),
        P(),
        P(),
        P(),
        P(),
        P(),
        P(),
        P(),
        P("seq", None, None),
        P(),
        P("seq"),
        P("samp", "seq", None),
    )
    return jax.shard_map(
        on_device,
        mesh=mesh,
        in_specs=placed,
        out_specs=(
            P("samp", "seq", None),
            P("samp", "seq", None),
            P(),
            P(),
            P(),
            P(),
            P(),
            P(),
            P(),
            P(),
        ),
        check_vma=False,
    )
```

```python
import jax
import jax.numpy as jnp
from jax import lax
from jax.experimental import pallas as pl
from jax.experimental.pallas import tpu as pltpu
from jax.sharding import PartitionSpec as P

HEADS = 4
QBLK = 32
KWIN = 128
TOK_DEV = 48
RIM = (KWIN - QBLK) // 2
D = 128
CP = 16

epsilon = 1e-05
LOG2E = 1.4426950408889634
LN2 = 0.6931471805599453
SCALING = 32.0 ** -0.5
F32 = jnp.float32
BF16 = jnp.bfloat16
OUT_AT = 4
TAIL_AT = 11 * D
ACC_ROWS = TAIL_AT + 64
GROUP = 4
PLAN = {"ln": "line", "fwd": "line", "tok": "line", "post": "line", "pool": "line", "bwd": "block"}
FINISH_PIECES = 3
VMEM_LIMIT = 56 * 1024 * 1024


def dot(a, b):
    return lax.dot_general(a, b, (((1,), (0,)), ((), ())), preferred_element_type=F32)


def dot_t(a, b):
    return lax.dot_general(a, b, (((1,), (1,)), ((), ())), preferred_element_type=F32)


def t_dot(a, b):
    return lax.dot_general(a, b, (((0,), (0,)), ((), ())), preferred_element_type=F32)


def iota(shape, dim):
    return lax.broadcasted_iota(jnp.int32, shape, dim)


def live_counts(counts_ref):
    shard = lax.axis_index("seq")
    last = counts_ref.shape[0] - 1
    left = jnp.where(shard > 0, counts_ref[jnp.maximum(shard - 1, 0)], 0)
    right = jnp.where(shard < last, counts_ref[jnp.minimum(shard + 1, last)], 0)
    return left, counts_ref[shard], right


def bias_kernel(counts_ref, pair_ref, wpair_ref, bias_ref, w_scr):
    rows = pair_ref.shape[0]
    span = w_scr.shape[1]
    key_of_row = iota((KWIN, CP, span), 0)
    key_of_lane = iota((KWIN, CP, span), 2) % KWIN
    w_pair = wpair_ref[...].astype(F32)
    wcol = jnp.concatenate(
        [jnp.broadcast_to(w_pair[:, h : h + 1], (CP, KWIN)) for h in range(HEADS)], axis=1
    )
    wide = jnp.broadcast_to(wcol[None], (KWIN, CP, span))
    w_scr[...] = (
        jnp.where(key_of_row == key_of_lane, wide, 0.0).astype(BF16).reshape(KWIN * CP, span)
    )
    left, own, right = live_counts(counts_ref)
    step = 128
    for r0 in range(0, rows, step):
        out = dot(pair_ref[r0 : r0 + step, :], w_scr[...])
        for q0 in range(0, step, QBLK):
            b = (r0 + q0) // QBLK
            slot = iota((1, KWIN), 1) + (b * QBLK - RIM)
            before, after = slot < 0, slot >= rows
            limit = jnp.where(before, left, jnp.where(after, right, own))
            place = jnp.where(before, slot + rows, jnp.where(after, slot - rows, slot))
            shift = jnp.where(place < limit, 0.0, -jnp.inf)
            for h in range(HEADS):
                bias_ref[b, h * QBLK : (h + 1) * QBLK, :] = (
                    out[q0 : q0 + QBLK, h * KWIN : (h + 1) * KWIN] * LOG2E + shift
                )


def pair_bias_call(counts, pair, w_pair):
    blocks = pair.shape[0] // QBLK
    return pl.pallas_call(
        bias_kernel,
        out_shape=jax.ShapeDtypeStruct((blocks, HEADS * QBLK, KWIN), F32),
        in_specs=[
            pl.BlockSpec(memory_space=pltpu.SMEM),
            pl.BlockSpec(memory_space=pltpu.VMEM),
            pl.BlockSpec(memory_space=pltpu.VMEM),
        ],
        out_specs=pl.BlockSpec(memory_space=pltpu.VMEM),
        scratch_shapes=[pltpu.VMEM((KWIN * CP, HEADS * KWIN), BF16)],
        compiler_params=pltpu.CompilerParams(vmem_limit_bytes=VMEM_LIMIT),
        cost_estimate=pl.CostEstimate(
            flops=2 * pair.shape[0] * KWIN * CP * HEADS * KWIN,
            bytes_accessed=5 << 20,
            transcendentals=0,
        ),
        name="pair_bias",
    )(counts, pair, w_pair)


def pair_grad_kernel(pair_ref, score_ref, out_ref, g_scr):
    blocks = score_ref.shape[0]
    wide = KWIN * CP
    key_of_lane = iota((KWIN, wide), 1) // CP
    own_key = key_of_lane == iota((KWIN, wide), 0)
    rows = []
    for h in range(HEADS):
        for b in range(blocks):
            g_scr[b * QBLK : (b + 1) * QBLK, :] = score_ref[
                b, h * QBLK : (h + 1) * QBLK, :
            ].astype(BF16)
        prod = t_dot(g_scr[...], pair_ref[...])
        rows.append(jnp.sum(jnp.where(own_key, prod, 0.0), axis=0, keepdims=True))
    stacked = jnp.concatenate(rows + [jnp.zeros((8 - HEADS, wide), F32)], axis=0)
    out_ref[...] = stacked


def pair_grad_call(pair, score_sum):
    return pl.pallas_call(
        pair_grad_kernel,
        out_shape=jax.ShapeDtypeStruct((8, KWIN * CP), F32),
        in_specs=[pl.BlockSpec(memory_space=pltpu.VMEM)] * 2,
        out_specs=pl.BlockSpec(memory_space=pltpu.VMEM),
        scratch_shapes=[pltpu.VMEM((pair.shape[0], KWIN), BF16)],
        compiler_params=pltpu.CompilerParams(vmem_limit_bytes=VMEM_LIMIT),
        cost_estimate=pl.CostEstimate(
            flops=2 * pair.shape[0] * KWIN * CP * HEADS * KWIN,
            bytes_accessed=3 << 20,
            transcendentals=0,
        ),
        name="pair_grad",
    )(pair, score_sum)


def layer_norm(x):
    mean = jnp.mean(x, axis=-1, keepdims=True)
    centred = x - mean
    variance = jnp.mean(centred * centred, axis=-1, keepdims=True)
    inv_std = lax.rsqrt(variance + epsilon)
    return centred * inv_std, inv_std


def ln_backward(gh, gain, normed, inv_std):
    gn = gh * gain
    return inv_std * (
        gn
        - jnp.mean(gn, axis=-1, keepdims=True)
        - normed * jnp.mean(gn * normed, axis=-1, keepdims=True)
    )


def pick_heads(o):
    head = iota((QBLK, D), 1) // (D // HEADS)
    r = o[0:QBLK]
    for h in range(1, HEADS):
        r = jnp.where(head == h, o[h * QBLK : (h + 1) * QBLK], r)
    return r


def aligned(x, n):
    return x if isinstance(x, int) else pl.multiple_of(x, n)


def section(name, step, count, body):
    def unrolled():
        for i in range(count):
            body(i)

    if PLAN[name] == "loop":
        pl.loop(0, count)(body)
    elif PLAN[name] == "block":
        pl.when(step >= 0)(unrolled)
    else:
        unrolled()


def main_kernel(
    counts_ref,
    memb_ref,
    atoms_ref,
    low_ref,
    high_ref,
    cot_ref,
    gain_ref,
    wq_ref,
    wk_ref,
    wv_ref,
    wg_ref,
    wout_ref,
    wtok_ref,
    bias_ref,
    pooled_ref,
    gqg_ref,
    gkv_ref,
    gu_ref,
    sendlow_ref,
    sendhigh_ref,
    acc_ref,
    score_ref,
    wqg,
    wkv,
    mem_t,
    mem2,
    inv_scr,
    hid,
    k_ext,
    v1,
    q_scr,
    sig_scr,
    att_scr,
    rden_scr,
    q4_scr,
    e_scr,
    upd_scr,
    act_scr,
    gpre_scr,
    g_scr,
    nga_scr,
    gkv_ext,
    open_scr,
    cot2,
):
    rows = atoms_ref.shape[1]
    ext = rows + 2 * RIM
    blocks = rows // QBLK
    step = pl.program_id(0)
    mask4 = (
        (iota((HEADS * QBLK, D), 0) // QBLK == iota((HEADS * QBLK, D), 1) // (D // HEADS))
        .astype(F32)
        .astype(BF16)
    )

    @pl.when(step == 0)
    def _():
        acc_ref[...] = jnp.zeros_like(acc_ref)
        wqg[:, 0:D] = wq_ref[...]
        wqg[:, D:] = wg_ref[...]
        wkv[:, 0:D] = wk_ref[...]
        wkv[:, D:] = wv_ref[...]
        score_ref[...] = jnp.zeros_like(score_ref)
        v1[:, D:] = jnp.ones((ext, D), BF16)
        shard = lax.axis_index("seq")
        own, first = counts_ref[shard], shard * TOK_DEV
        local = memb_ref[...] - first
        slot = iota((D, rows), 1)
        hit = (local == iota((D, rows), 0)) & (slot < own)
        hit_f = jnp.where(hit, 1.0, 0.0)
        total = jnp.sum(hit_f, axis=1, keepdims=True)
        inv = 1.0 / jnp.maximum(total, 1.0)
        mem_t[...] = hit_f[0:TOK_DEV].astype(BF16)
        inv_scr[...] = jnp.broadcast_to(inv[0:TOK_DEV], inv_scr.shape)
        weighted = hit_f * inv
        high = weighted.astype(BF16)
        rest = (weighted - high.astype(F32)).astype(BF16)
        mem2[:, 0:TOK_DEV] = high.astype(F32).T.astype(BF16)[:, 0:TOK_DEV]
        mem2[:, TOK_DEV : 2 * TOK_DEV] = rest.astype(F32).T.astype(BF16)[:, 0:TOK_DEV]

    gain = gain_ref[...]
    fwd_size = blocks if PLAN["fwd"] != "loop" else GROUP
    bwd_size = blocks if PLAN["bwd"] != "loop" else GROUP
    def project(src, at, from_row, size):
        x = src[0, pl.ds(from_row, size), :].astype(F32)
        normed, _ = layer_norm(x)
        hidden = (normed * gain).astype(BF16)
        kv = dot(hidden, wkv[...]).astype(BF16)
        to = pl.ds(at, size)
        k_ext[to, :] = kv[:, 0:D]
        v1[to, 0:D] = kv[:, D:]
        hid[to, :] = hidden
        return hidden

    size = 128
    project(low_ref, 0, 0, RIM)
    project(high_ref, RIM + rows, 0, RIM)

    def ln_rows(c):
        c0 = aligned(c * size, size)
        hidden = project(atoms_ref, aligned(c0 + RIM, 16), c0, size)
        qg = dot(hidden, wqg[...])
        q_scr[pl.ds(c0, size), :] = (qg[:, 0:D] * (SCALING * LOG2E)).astype(BF16)
        sig_scr[pl.ds(c0, size), :] = 0.5 * jnp.tanh(0.5 * qg[:, D:]) + 0.5

    section("ln", step, rows // size, ln_rows)

    def fwd_group(g):
        for w in range(fwd_size):
            b = g * fwd_size + w
            r0 = aligned(b * QBLK, QBLK)
            q_b = q_scr[pl.ds(r0, QBLK), :]
            q4 = jnp.concatenate([q_b] * HEADS, axis=0) * mask4
            q4_scr[b] = q4
            scores = dot_t(q4, k_ext[pl.ds(r0, KWIN), :]) + bias_ref[b]
            e = jnp.exp2(scores).astype(BF16)
            e_scr[b] = e
            o = dot(e, v1[pl.ds(r0, KWIN), :])
            num = pick_heads(o[:, 0:D])
            rden = 1.0 / pick_heads(o[:, D:])
            att_scr[pl.ds(r0, QBLK), :] = num * rden
            rden_scr[pl.ds(r0, QBLK), :] = rden

    section("fwd", step, blocks // fwd_size, fwd_group)

    cot2[0:TOK_DEV, :] = cot_ref[0]
    cot2[TOK_DEV:, :] = cot_ref[0]
    cols = 256
    width = wtok_ref.shape[1]

    def tok_rows(c):
        sl = pl.ds(aligned(c * size, size), size)
        gated = (sig_scr[sl, :] * att_scr[sl, :]).astype(BF16)
        upd = (atoms_ref[0, sl, :].astype(F32) + dot(gated, wout_ref[...])).astype(BF16)
        upd_scr[sl, :] = upd
        for t0 in range(0, width, cols):
            cs = slice(t0, t0 + cols)
            pre = dot(upd, wtok_ref[:, cs])
            sg = 0.5 * jnp.tanh(0.5 * pre) + 0.5
            act = pre * sg
            act_scr[sl, cs] = act.astype(BF16)
            grad_act = dot(mem2[sl, :], cot2[:, cs])
            gpre_scr[sl, cs] = (grad_act * (sg + act * (1.0 - sg))).astype(BF16)

    section("tok", step, rows // size, tok_rows)

    def post_rows(c):
        sl = pl.ds(aligned(c * size, size), size)
        gu = dot_t(gpre_scr[sl, :], wtok_ref[...]).astype(BF16)
        gu_ref[0, sl, :] = gu
        sig = sig_scr[sl, :]
        att = att_scr[sl, :]
        gated = (sig * att).astype(BF16)
        acc_ref[OUT_AT * D : (OUT_AT + 1) * D, :] += t_dot(gated, gu)
        gatt = dot_t(gu, wout_ref[...]) * sig
        gatt_att = gatt * att
        gqg_ref[0, sl, D:] = (gatt_att * (1.0 - sig)).astype(BF16)
        rden = rden_scr[sl, :]
        g_scr[sl, :] = (gatt * rden).astype(BF16)
        nga_scr[sl, :] = (-(gatt_att * rden)).astype(BF16)

    section("post", step, rows // size, post_rows)

    def pool_cols(c):
        t0 = c * cols
        cs = slice(t0, t0 + cols)
        pooled_ref[0, :, cs] = (
            dot(mem_t[...], act_scr[:, cs]) * jnp.concatenate([inv_scr[...]] * (cols // D), axis=1)
        ).astype(BF16)
        grad_tok = t_dot(upd_scr[...], gpre_scr[:, cs])
        for t1 in range(0, cols, D):
            at = (OUT_AT + 1) * D + t0 + t1
            acc_ref[at : at + D, :] += grad_tok[:, t1 : t1 + D]

    section("pool", step, width // cols, pool_cols)

    spans = KWIN // QBLK
    open_scr[...] = jnp.zeros_like(open_scr)

    def bwd_group(g):
        open_k = [open_scr[0, t * QBLK : (t + 1) * QBLK, :] for t in range(spans - 1)]
        open_v = [open_scr[1, t * QBLK : (t + 1) * QBLK, :] for t in range(spans - 1)]
        for w in range(bwd_size):
            b = g * bwd_size + w
            r0 = aligned(b * QBLK, QBLK)
            g4 = jnp.concatenate([g_scr[pl.ds(r0, QBLK), :]] * HEADS, axis=0) * mask4
            nga4 = jnp.concatenate([nga_scr[pl.ds(r0, QBLK), :]] * HEADS, axis=0) * mask4
            e = e_scr[b]
            dp = dot_t(jnp.concatenate([g4, nga4], axis=1), v1[pl.ds(r0, KWIN), :])
            ds = e.astype(F32) * dp
            score_ref[b] += ds
            dsl = ds.astype(BF16)
            gq = pick_heads(dot(dsl, k_ext[pl.ds(r0, KWIN), :]))
            gqg_ref[0, pl.ds(r0, QBLK), 0:D] = (gq * SCALING).astype(BF16)
            gk = t_dot(dsl, q4_scr[b])
            gv = t_dot(e, g4)
            part_k = [gk[t * QBLK : (t + 1) * QBLK] for t in range(spans)]
            part_v = [gv[t * QBLK : (t + 1) * QBLK] for t in range(spans)]
            open_k = [x + y for x, y in zip(open_k, part_k)] + part_k[len(open_k) :]
            open_v = [x + y for x, y in zip(open_v, part_v)] + part_v[len(open_v) :]
            gkv_ext[pl.ds(r0, QBLK), 0:D] = (open_k[0] * LN2).astype(BF16)
            gkv_ext[pl.ds(r0, QBLK), D:] = open_v[0].astype(BF16)
            open_k, open_v = open_k[1:], open_v[1:]
        for t in range(spans - 1):
            open_scr[0, t * QBLK : (t + 1) * QBLK, :] = open_k[t]
            open_scr[1, t * QBLK : (t + 1) * QBLK, :] = open_v[t]

    section("bwd", step, blocks // bwd_size, bwd_group)
    gkv_ext[rows:, 0:D] = (open_scr[0] * LN2).astype(BF16)
    gkv_ext[rows:, D:] = open_scr[1].astype(BF16)
    sendlow_ref[0] = gkv_ext[0:RIM, :]
    sendhigh_ref[0] = gkv_ext[RIM + rows :, :]
    gkv_ref[0] = gkv_ext[RIM : RIM + rows, :]
    grad_qg = t_dot(hid[RIM : RIM + rows, :], gqg_ref[0])
    grad_kv = t_dot(hid[...], gkv_ext[...])
    for at, part in ((0, grad_qg[:, 0:D]), (1, grad_kv[:, 0:D]), (2, grad_kv[:, D:]), (3, grad_qg[:, D:])):
        acc_ref[at * D : (at + 1) * D, :] += part

    @pl.when(step == pl.num_programs(0) - 1)
    def _():
        terms = jnp.zeros((D, D), F32)
        for at, w_ref in enumerate((wq_ref, wk_ref, wv_ref, wg_ref)):
            terms += acc_ref[at * D : (at + 1) * D, :] * w_ref[...].astype(F32)
        by_channel = jnp.broadcast_to(jnp.sum(terms, axis=1, keepdims=True), (D, D)).T
        acc_ref[TAIL_AT : TAIL_AT + 8, :] = jnp.where(
            iota((8, D), 0) == 0, by_channel[0:8] / gain, 0.0
        )


def main_call(counts, memb, atoms, low, high, cot, gain, wq, wk, wv, wg, wout, wtok, bias):
    samples, rows, _ = atoms.shape
    ext = rows + 2 * RIM
    width = wtok.shape[1]
    blocks = rows // QBLK
    hq = HEADS * QBLK

    def per_sample(*shape):
        return pl.BlockSpec((1,) + shape, lambda s: (s,) + (0,) * len(shape))

    def whole(*shape):
        return pl.BlockSpec(shape, lambda s: (0,) * len(shape))

    sd = jax.ShapeDtypeStruct
    return pl.pallas_call(
        main_kernel,
        grid=(samples,),
        out_shape=(
            sd((samples, TOK_DEV, width), BF16),
            sd((samples, rows, 2 * D), BF16),
            sd((samples, rows, 2 * D), BF16),
            sd((samples, rows, D), BF16),
            sd((samples, RIM, 2 * D), BF16),
            sd((samples, RIM, 2 * D), BF16),
            sd((ACC_ROWS, D), F32),
            sd((blocks, hq, KWIN), F32),
        ),
        in_specs=[
            pl.BlockSpec(memory_space=pltpu.SMEM),
            whole(1, rows),
            per_sample(rows, D),
            per_sample(RIM, D),
            per_sample(RIM, D),
            per_sample(TOK_DEV, width),
            whole(1, D),
            whole(D, D),
            whole(D, D),
            whole(D, D),
            whole(D, D),
            whole(D, D),
            whole(D, width),
            whole(blocks, hq, KWIN),
        ],
        out_specs=(
            per_sample(TOK_DEV, width),
            per_sample(rows, 2 * D),
            per_sample(rows, 2 * D),
            per_sample(rows, D),
            per_sample(RIM, 2 * D),
            per_sample(RIM, 2 * D),
            whole(ACC_ROWS, D),
            whole(blocks, hq, KWIN),
        ),
        scratch_shapes=[
            pltpu.VMEM((D, 2 * D), BF16),
            pltpu.VMEM((D, 2 * D), BF16),
            pltpu.VMEM((TOK_DEV, rows), BF16),
            pltpu.VMEM((rows, 2 * TOK_DEV), BF16),
            pltpu.VMEM((TOK_DEV, D), F32),
            pltpu.VMEM((ext, D), BF16),
            pltpu.VMEM((ext, D), BF16),
            pltpu.VMEM((ext, 2 * D), BF16),
            pltpu.VMEM((rows, D), BF16),
            pltpu.VMEM((rows, D), F32),
            pltpu.VMEM((rows, D), F32),
            pltpu.VMEM((rows, D), F32),
            pltpu.VMEM((blocks, hq, D), BF16),
            pltpu.VMEM((blocks, hq, KWIN), BF16),
            pltpu.VMEM((rows, D), BF16),
            pltpu.VMEM((rows, width), BF16),
            pltpu.VMEM((rows, width), BF16),
            pltpu.VMEM((rows, D), BF16),
            pltpu.VMEM((rows, D), BF16),
            pltpu.VMEM((ext, 2 * D), BF16),
            pltpu.VMEM((2, 2 * RIM, D), F32),
            pltpu.VMEM((2 * TOK_DEV, width), BF16),
        ],
        compiler_params=pltpu.CompilerParams(
            vmem_limit_bytes=VMEM_LIMIT, dimension_semantics=("arbitrary",)
        ),
        name="atom_layer",
    )(counts, memb, atoms, low, high, cot, gain, wq, wk, wv, wg, wout, wtok, bias)


def finish_kernel(
    atoms_ref, gqg_ref, gkv_ref, gu_ref, left_ref, right_ref, gain_ref, wq_ref, wk_ref, wv_ref, wg_ref, *rest
):
    gatoms_ref, gkv = rest[-2], rest[-1]
    rows = atoms_ref.shape[1]
    gain = gain_ref[...]
    wqg = jnp.concatenate([wq_ref[...], wg_ref[...]], axis=1)
    wkv = jnp.concatenate([wk_ref[...], wv_ref[...]], axis=1)
    gkv[...] = gkv_ref[0]
    gkv[0:RIM, :] = (gkv[0:RIM, :].astype(F32) + left_ref[0].astype(F32)).astype(BF16)
    gkv[rows - RIM :, :] = (gkv[rows - RIM :, :].astype(F32) + right_ref[0].astype(F32)).astype(BF16)
    size = 128
    for c0 in range(0, rows, size):
        sl = slice(c0, c0 + size)
        gh = dot_t(gqg_ref[0, sl, :], wqg) + dot_t(gkv[sl, :], wkv)
        normed, inv_std = layer_norm(atoms_ref[0, sl, :].astype(F32))
        ga = gu_ref[0, sl, :].astype(F32) + ln_backward(gh, gain, normed, inv_std)
        gatoms_ref[0, sl, :] = ga.astype(BF16)


def finish_call(first, number, atoms, gqg, gkv, gu, from_left, from_right, gain, ws, held):
    samples, rows, _ = atoms.shape

    def per_sample(*shape):
        return pl.BlockSpec((1,) + shape, lambda s: (s + first,) + (0,) * len(shape))

    def whole(*shape):
        return pl.BlockSpec(shape, lambda s: (0,) * len(shape))

    specs = [
        per_sample(rows, D),
        per_sample(rows, 2 * D),
        per_sample(rows, 2 * D),
        per_sample(rows, D),
        per_sample(RIM, 2 * D),
        per_sample(RIM, 2 * D),
        whole(1, D),
    ] + [whole(D, D)] * 4
    operands = [atoms, gqg, gkv, gu, from_left, from_right, gain, *ws]
    aliases = {}
    if held is not None:
        specs.append(pl.BlockSpec(memory_space=pl.ANY))
        aliases = {len(operands): 0}
        operands.append(held)
    return pl.pallas_call(
        finish_kernel,
        grid=(number,),
        out_shape=jax.ShapeDtypeStruct(atoms.shape, BF16),
        in_specs=specs,
        out_specs=per_sample(rows, D),
        scratch_shapes=[pltpu.VMEM((rows, 2 * D), BF16)],
        input_output_aliases=aliases,
        compiler_params=pltpu.CompilerParams(dimension_semantics=("arbitrary",)),
        cost_estimate=pl.CostEstimate(
            flops=number * rows * D * 4 * D * 2,
            bytes_accessed=number * rows * D * 14,
            transcendentals=0,
        ),
        name="finish",
    )(*operands)


def route(count, digits, k):
    out = []
    total = 1
    for _, size in digits:
        total *= size
    for i in range(count):
        c, m = 0, 1
        for stride, size in digits:
            c += (i // stride % size) * m
            m *= size
        q = (c + k) % total
        j = i
        for stride, size in digits:
            j += (q % size - i // stride % size) * stride
            q //= size
        out.append((i, j))
    return out


def group_size(digits):
    total = 1
    for _, size in digits:
        total *= size
    return total


def exchange_sum(x, axis, digits):
    count = lax.axis_size(axis)
    low = x.astype(BF16)
    total = low.astype(F32)
    for k in range(1, group_size(digits)):
        total = total + lax.ppermute(low, axis, route(count, digits, k)).astype(F32)
    return total


def scatter_sum(x, axis):
    count = lax.axis_size(axis)
    me = lax.axis_index(axis)
    size = x.shape[0] // count
    low = x.astype(BF16)
    total = lax.dynamic_slice_in_dim(x, me * size, size, 0)
    for k in range(1, count):
        piece = lax.dynamic_slice_in_dim(low, (me + k) % count * size, size, 0)
        total = total + lax.ppermute(piece, axis, route(count, [(1, count)], k)).astype(F32)
    return total


def gather(x, axis):
    count = lax.axis_size(axis)
    me = lax.axis_index(axis)
    size = x.shape[0]
    low = x.astype(BF16)
    out = jnp.zeros((count * size,) + x.shape[1:], BF16)
    out = lax.dynamic_update_slice_in_dim(out, low, me * size, 0)
    for k in range(1, count):
        piece = lax.ppermute(low, axis, route(count, [(1, count)], k))
        out = lax.dynamic_update_slice_in_dim(out, piece, (me - k) % count * size, 0)
    return out


def seq_stages(count):
    stages, stride = [], 1
    while stride < count:
        size = min(4, count // stride)
        stages.append([(stride, size)])
        stride *= size
    return stages


def shifted(block, axis, distance):
    devices = range(lax.axis_size(axis))
    moves = [(i - distance, i) for i in devices if i - distance in devices]
    return lax.ppermute(block, axis, moves)


def on_device(
    atoms,
    gain,
    w_query,
    w_key,
    w_value,
    w_gate,
    w_out,
    w_token,
    w_pair,
    pair_cond,
    counts,
    membership,
    pooled_cot,
):
    samples, rows, _ = atoms.shape
    low = shifted(atoms[:, rows - RIM :], "seq", 1)
    high = shifted(atoms[:, :RIM], "seq", -1)
    pair = pair_cond.reshape(rows, KWIN * CP)
    bias = pair_bias_call(counts, pair, w_pair)
    gain_row = gain.reshape(1, D)
    ws = (w_query, w_key, w_value, w_gate)
    pooled, gqg, gkv, gu, send_low, send_high, acc, score_sum = main_call(
        counts,
        membership.reshape(1, rows),
        atoms,
        low,
        high,
        pooled_cot,
        gain_row,
        *ws,
        w_out,
        w_token,
        bias,
    )
    total = scatter_sum(acc, "samp")
    from_right = shifted(send_low, "seq", -1)
    from_left = shifted(send_high, "seq", 1)
    pair_part = pair_grad_call(pair, score_sum)
    pair_sum = jnp.sum(pair_part[:HEADS].reshape(HEADS, KWIN, CP), axis=1).reshape(1, HEADS * CP)
    pair_rows = jnp.pad(pair_sum, ((0, 15), (0, D - HEADS * CP)))
    main_rows = total.shape[0]
    total = jnp.concatenate([total, pair_rows], axis=0)
    total, from_left, from_right = lax.optimization_barrier((total, from_left, from_right))
    grad_atoms = None
    share = samples // FINISH_PIECES
    for at, digits in enumerate(seq_stages(lax.axis_size("seq"))):
        if at < FINISH_PIECES:
            grad_atoms = finish_call(
                at * share, share, atoms, gqg, gkv, gu, from_left, from_right, gain_row, ws, grad_atoms
            )
        total = exchange_sum(total, "seq", digits)
        total, grad_atoms = lax.optimization_barrier((total, grad_atoms))
    for at in range(len(seq_stages(lax.axis_size("seq"))), FINISH_PIECES):
        grad_atoms = finish_call(
            at * share, share, atoms, gqg, gkv, gu, from_left, from_right, gain_row, ws, grad_atoms
        )
    parts = gather(total, "samp").astype(F32).reshape(-1, main_rows + 16, D)
    tail = jnp.sum(parts[:, main_rows:], axis=0)
    flat = parts[:, :main_rows].reshape(-1, D)
    width = w_token.shape[1]
    mats = [flat[i * D : (i + 1) * D] for i in range(5 + width // D)]
    gain_total = flat[TAIL_AT]
    grad_pair = tail[0, : HEADS * CP].reshape(HEADS, CP).T
    return (
        pooled,
        grad_atoms,
        gain_total,
        mats[0],
        mats[1],
        mats[2],
        mats[3],
        mats[4],
        jnp.concatenate(mats[5:], axis=1),
        grad_pair,
    )


def solution(mesh):
    placed = (
        P("samp", "seq", None),
        P(),
        P(),
        P(),
        P(),
        P(),
        P(),
        P(),
        P(),
        P("seq", None, None),
        P(),
        P("seq"),
        P("samp", "seq", None),
    )
    return jax.shard_map(
        on_device,
        mesh=mesh,
        in_specs=placed,
        out_specs=(
            P("samp", "seq", None),
            P("samp", "seq", None),
            P(),
            P(),
            P(),
            P(),
            P(),
            P(),
            P(),
            P(),
        ),
        check_vma=False,
    )
```

```python
import jax
import jax.numpy as jnp
from jax import lax
from jax.experimental import pallas as pl
from jax.experimental.pallas import tpu as pltpu
from jax.sharding import PartitionSpec as P

HEADS = 4
QBLK = 32
KWIN = 128
TOK_DEV = 48
RIM = (KWIN - QBLK) // 2
D = 128
CP = 16

epsilon = 1e-05
LOG2E = 1.4426950408889634
LN2 = 0.6931471805599453
SCALING = 32.0 ** -0.5
F32 = jnp.float32
BF16 = jnp.bfloat16
OUT_AT = 4
TAIL_AT = 11 * D
ACC_ROWS = TAIL_AT + 64
GROUP = 4
PLAN = {"ln": "line", "fwd": "line", "tok": "line", "post": "line", "pool": "line", "bwd": "block"}
RADIX = (4, 4, 4)
FINISH_PIECES = 3
FINISH_LATE = 1
VMEM_LIMIT = 56 * 1024 * 1024


def dot(a, b):
    return lax.dot_general(a, b, (((1,), (0,)), ((), ())), preferred_element_type=F32)


def dot_t(a, b):
    return lax.dot_general(a, b, (((1,), (1,)), ((), ())), preferred_element_type=F32)


def t_dot(a, b):
    return lax.dot_general(a, b, (((0,), (0,)), ((), ())), preferred_element_type=F32)


def iota(shape, dim):
    return lax.broadcasted_iota(jnp.int32, shape, dim)


def live_counts(counts_ref):
    shard = lax.axis_index("seq")
    last = counts_ref.shape[0] - 1
    left = jnp.where(shard > 0, counts_ref[jnp.maximum(shard - 1, 0)], 0)
    right = jnp.where(shard < last, counts_ref[jnp.minimum(shard + 1, last)], 0)
    return left, counts_ref[shard], right


def bias_kernel(counts_ref, pair_ref, wpair_ref, bias_ref, w_scr):
    rows = pair_ref.shape[0]
    span = w_scr.shape[1]
    key_of_row = iota((KWIN, CP, span), 0)
    key_of_lane = iota((KWIN, CP, span), 2) % KWIN
    w_pair = wpair_ref[...].astype(F32)
    wcol = jnp.concatenate(
        [jnp.broadcast_to(w_pair[:, h : h + 1], (CP, KWIN)) for h in range(HEADS)], axis=1
    )
    wide = jnp.broadcast_to(wcol[None], (KWIN, CP, span))
    w_scr[...] = (
        jnp.where(key_of_row == key_of_lane, wide, 0.0).astype(BF16).reshape(KWIN * CP, span)
    )
    left, own, right = live_counts(counts_ref)
    step = 128
    for r0 in range(0, rows, step):
        out = dot(pair_ref[r0 : r0 + step, :], w_scr[...])
        for q0 in range(0, step, QBLK):
            b = (r0 + q0) // QBLK
            slot = iota((1, KWIN), 1) + (b * QBLK - RIM)
            before, after = slot < 0, slot >= rows
            limit = jnp.where(before, left, jnp.where(after, right, own))
            place = jnp.where(before, slot + rows, jnp.where(after, slot - rows, slot))
            shift = jnp.where(place < limit, 0.0, -jnp.inf)
            for h in range(HEADS):
                bias_ref[b, h * QBLK : (h + 1) * QBLK, :] = (
                    out[q0 : q0 + QBLK, h * KWIN : (h + 1) * KWIN] * LOG2E + shift
                )


def pair_bias_call(counts, pair, w_pair):
    blocks = pair.shape[0] // QBLK
    return pl.pallas_call(
        bias_kernel,
        out_shape=jax.ShapeDtypeStruct((blocks, HEADS * QBLK, KWIN), F32),
        in_specs=[
            pl.BlockSpec(memory_space=pltpu.SMEM),
            pl.BlockSpec(memory_space=pltpu.VMEM),
            pl.BlockSpec(memory_space=pltpu.VMEM),
        ],
        out_specs=pl.BlockSpec(memory_space=pltpu.VMEM),
        scratch_shapes=[pltpu.VMEM((KWIN * CP, HEADS * KWIN), BF16)],
        compiler_params=pltpu.CompilerParams(vmem_limit_bytes=VMEM_LIMIT),
        cost_estimate=pl.CostEstimate(
            flops=2 * pair.shape[0] * KWIN * CP * HEADS * KWIN,
            bytes_accessed=5 << 20,
            transcendentals=0,
        ),
        name="pair_bias",
    )(counts, pair, w_pair)


def pair_grad_kernel(pair_ref, score_ref, out_ref, g_scr):
    blocks = score_ref.shape[0]
    wide = KWIN * CP
    key_of_lane = iota((KWIN, wide), 1) // CP
    own_key = key_of_lane == iota((KWIN, wide), 0)
    rows = []
    for h in range(HEADS):
        for b in range(blocks):
            g_scr[b * QBLK : (b + 1) * QBLK, :] = score_ref[
                b, h * QBLK : (h + 1) * QBLK, :
            ].astype(BF16)
        prod = t_dot(g_scr[...], pair_ref[...])
        rows.append(jnp.sum(jnp.where(own_key, prod, 0.0), axis=0, keepdims=True))
    stacked = jnp.concatenate(rows + [jnp.zeros((8 - HEADS, wide), F32)], axis=0)
    out_ref[...] = stacked


def pair_grad_call(pair, score_sum):
    return pl.pallas_call(
        pair_grad_kernel,
        out_shape=jax.ShapeDtypeStruct((8, KWIN * CP), F32),
        in_specs=[pl.BlockSpec(memory_space=pltpu.VMEM)] * 2,
        out_specs=pl.BlockSpec(memory_space=pltpu.VMEM),
        scratch_shapes=[pltpu.VMEM((pair.shape[0], KWIN), BF16)],
        compiler_params=pltpu.CompilerParams(vmem_limit_bytes=VMEM_LIMIT),
        cost_estimate=pl.CostEstimate(
            flops=2 * pair.shape[0] * KWIN * CP * HEADS * KWIN,
            bytes_accessed=3 << 20,
            transcendentals=0,
        ),
        name="pair_grad",
    )(pair, score_sum)


def layer_norm(x):
    mean = jnp.mean(x, axis=-1, keepdims=True)
    centred = x - mean
    variance = jnp.mean(centred * centred, axis=-1, keepdims=True)
    inv_std = lax.rsqrt(variance + epsilon)
    return centred * inv_std, inv_std


def ln_backward(gh, gain, normed, inv_std):
    gn = gh * gain
    return inv_std * (
        gn
        - jnp.mean(gn, axis=-1, keepdims=True)
        - normed * jnp.mean(gn * normed, axis=-1, keepdims=True)
    )


def pick_heads(o):
    head = iota((QBLK, D), 1) // (D // HEADS)
    r = o[0:QBLK]
    for h in range(1, HEADS):
        r = jnp.where(head == h, o[h * QBLK : (h + 1) * QBLK], r)
    return r


def aligned(x, n):
    return x if isinstance(x, int) else pl.multiple_of(x, n)


def section(name, step, count, body):
    def unrolled():
        for i in range(count):
            body(i)

    if PLAN[name] == "loop":
        pl.loop(0, count)(body)
    elif PLAN[name] == "block":
        pl.when(step >= 0)(unrolled)
    else:
        unrolled()


def main_kernel(
    counts_ref,
    memb_ref,
    atoms_ref,
    low_ref,
    high_ref,
    cot_ref,
    gain_ref,
    wq_ref,
    wk_ref,
    wv_ref,
    wg_ref,
    wout_ref,
    wtok_ref,
    bias_ref,
    pooled_ref,
    gqg_ref,
    gkv_ref,
    gu_ref,
    sendlow_ref,
    sendhigh_ref,
    sum_ref,
    score_ref,
    wqg,
    wkv,
    wtok_t,
    wout_t,
    mem_t,
    mem2,
    inv_scr,
    hid,
    k_ext,
    v1,
    q_scr,
    sig_scr,
    att_scr,
    rden_scr,
    q4_scr,
    e_scr,
    upd_scr,
    act_scr,
    gpre_scr,
    g_scr,
    nga_scr,
    gkv_ext,
    open_scr,
    cot2,
    acc_ref,
):
    rows = atoms_ref.shape[1]
    ext = rows + 2 * RIM
    blocks = rows // QBLK
    step = pl.program_id(0)
    mask4 = (
        (iota((HEADS * QBLK, D), 0) // QBLK == iota((HEADS * QBLK, D), 1) // (D // HEADS))
        .astype(F32)
        .astype(BF16)
    )

    @pl.when(step == 0)
    def _():
        acc_ref[...] = jnp.zeros_like(acc_ref)
        wqg[:, 0:D] = wq_ref[...]
        wtok_t[...] = wtok_ref[...].astype(F32).T.astype(BF16)
        wout_t[...] = wout_ref[...].astype(F32).T.astype(BF16)
        wqg[:, D:] = wg_ref[...]
        wkv[:, 0:D] = wk_ref[...]
        wkv[:, D:] = wv_ref[...]
        score_ref[...] = jnp.zeros_like(score_ref)
        v1[:, D:] = jnp.ones((ext, D), BF16)
        shard = lax.axis_index("seq")
        own, first = counts_ref[shard], shard * TOK_DEV
        local = memb_ref[...] - first
        slot = iota((D, rows), 1)
        hit = (local == iota((D, rows), 0)) & (slot < own)
        hit_f = jnp.where(hit, 1.0, 0.0)
        total = jnp.sum(hit_f, axis=1, keepdims=True)
        inv = 1.0 / jnp.maximum(total, 1.0)
        mem_t[...] = hit_f[0:TOK_DEV].astype(BF16)
        inv_scr[...] = jnp.broadcast_to(inv[0:TOK_DEV], inv_scr.shape)
        weighted = hit_f * inv
        high = weighted.astype(BF16)
        rest = (weighted - high.astype(F32)).astype(BF16)
        mem2[:, 0:TOK_DEV] = high.astype(F32).T.astype(BF16)[:, 0:TOK_DEV]
        mem2[:, TOK_DEV : 2 * TOK_DEV] = rest.astype(F32).T.astype(BF16)[:, 0:TOK_DEV]

    gain = gain_ref[...]
    fwd_size = blocks if PLAN["fwd"] != "loop" else GROUP
    bwd_size = blocks if PLAN["bwd"] != "loop" else GROUP
    def project(src, at, from_row, size):
        x = src[0, pl.ds(from_row, size), :].astype(F32)
        normed, _ = layer_norm(x)
        hidden = (normed * gain).astype(BF16)
        kv = dot(hidden, wkv[...]).astype(BF16)
        to = pl.ds(at, size)
        k_ext[to, :] = kv[:, 0:D]
        v1[to, 0:D] = kv[:, D:]
        hid[to, :] = hidden
        return hidden

    size = 128
    project(low_ref, 0, 0, RIM)
    project(high_ref, RIM + rows, 0, RIM)

    def ln_rows(c):
        c0 = aligned(c * size, size)
        hidden = project(atoms_ref, aligned(c0 + RIM, 16), c0, size)
        qg = dot(hidden, wqg[...])
        q_scr[pl.ds(c0, size), :] = (qg[:, 0:D] * (SCALING * LOG2E)).astype(BF16)
        sig_scr[pl.ds(c0, size), :] = 0.5 * jnp.tanh(0.5 * qg[:, D:]) + 0.5

    section("ln", step, rows // size, ln_rows)

    def fwd_group(g):
        for w in range(fwd_size):
            b = g * fwd_size + w
            r0 = aligned(b * QBLK, QBLK)
            q_b = q_scr[pl.ds(r0, QBLK), :]
            q4 = jnp.concatenate([q_b] * HEADS, axis=0) * mask4
            q4_scr[b] = q4
            scores = dot_t(q4, k_ext[pl.ds(r0, KWIN), :]) + bias_ref[b]
            e = jnp.exp2(scores).astype(BF16)
            e_scr[b] = e
            o = dot(e, v1[pl.ds(r0, KWIN), :])
            num = pick_heads(o[:, 0:D])
            rden = 1.0 / pick_heads(o[:, D:])
            att_scr[pl.ds(r0, QBLK), :] = num * rden
            rden_scr[pl.ds(r0, QBLK), :] = rden

    section("fwd", step, blocks // fwd_size, fwd_group)

    cot2[0:TOK_DEV, :] = cot_ref[0]
    cot2[TOK_DEV:, :] = cot_ref[0]
    cols = 256
    width = wtok_ref.shape[1]

    def tok_rows(c):
        sl = pl.ds(aligned(c * 256, 256), 256)
        gated = (sig_scr[sl, :] * att_scr[sl, :]).astype(BF16)
        upd = (atoms_ref[0, sl, :].astype(F32) + dot(gated, wout_ref[...])).astype(BF16)
        upd_scr[sl, :] = upd
        for t0 in range(0, width, cols):
            cs = slice(t0, t0 + cols)
            pre = dot(upd, wtok_ref[:, cs])
            sg = 0.5 * jnp.tanh(0.5 * pre) + 0.5
            act = pre * sg
            act_scr[sl, cs] = act.astype(BF16)
            grad_act = dot(mem2[sl, :], cot2[:, cs])
            gpre_scr[sl, cs] = (grad_act * (sg + act * (1.0 - sg))).astype(BF16)

    section("tok", step, rows // 256, tok_rows)

    def post_rows(c):
        sl = pl.ds(aligned(c * 256, 256), 256)
        gu = dot(gpre_scr[sl, :], wtok_t[...]).astype(BF16)
        gu_ref[0, sl, :] = gu
        sig = sig_scr[sl, :]
        att = att_scr[sl, :]
        gated = (sig * att).astype(BF16)
        acc_ref[OUT_AT * D : (OUT_AT + 1) * D, :] += t_dot(gated, gu)
        gatt = dot(gu, wout_t[...]) * sig
        gatt_att = gatt * att
        gqg_ref[0, sl, D:] = (gatt_att * (1.0 - sig)).astype(BF16)
        rden = rden_scr[sl, :]
        g_scr[sl, :] = (gatt * rden).astype(BF16)
        nga_scr[sl, :] = (-(gatt_att * rden)).astype(BF16)

    section("post", step, rows // 256, post_rows)

    def pool_cols(c):
        t0 = c * cols
        cs = slice(t0, t0 + cols)
        pooled_ref[0, :, cs] = (
            dot(mem_t[...], act_scr[:, cs]) * jnp.concatenate([inv_scr[...]] * (cols // D), axis=1)
        ).astype(BF16)
        grad_tok = t_dot(upd_scr[...], gpre_scr[:, cs])
        for t1 in range(0, cols, D):
            at = (OUT_AT + 1) * D + t0 + t1
            acc_ref[at : at + D, :] += grad_tok[:, t1 : t1 + D]

    section("pool", step, width // cols, pool_cols)

    spans = KWIN // QBLK
    open_scr[...] = jnp.zeros_like(open_scr)

    def bwd_group(g):
        open_k = [open_scr[0, t * QBLK : (t + 1) * QBLK, :] for t in range(spans - 1)]
        open_v = [open_scr[1, t * QBLK : (t + 1) * QBLK, :] for t in range(spans - 1)]
        for w in range(bwd_size):
            b = g * bwd_size + w
            r0 = aligned(b * QBLK, QBLK)
            g4 = jnp.concatenate([g_scr[pl.ds(r0, QBLK), :]] * HEADS, axis=0) * mask4
            nga4 = jnp.concatenate([nga_scr[pl.ds(r0, QBLK), :]] * HEADS, axis=0) * mask4
            e = e_scr[b]
            dp = dot_t(jnp.concatenate([g4, nga4], axis=1), v1[pl.ds(r0, KWIN), :])
            ds = e.astype(F32) * dp
            score_ref[b] += ds
            dsl = ds.astype(BF16)
            gq = pick_heads(dot(dsl, k_ext[pl.ds(r0, KWIN), :]))
            gqg_ref[0, pl.ds(r0, QBLK), 0:D] = (gq * SCALING).astype(BF16)
            gk = t_dot(dsl, q4_scr[b])
            gv = t_dot(e, g4)
            part_k = [gk[t * QBLK : (t + 1) * QBLK] for t in range(spans)]
            part_v = [gv[t * QBLK : (t + 1) * QBLK] for t in range(spans)]
            open_k = [x + y for x, y in zip(open_k, part_k)] + part_k[len(open_k) :]
            open_v = [x + y for x, y in zip(open_v, part_v)] + part_v[len(open_v) :]
            gkv_ext[pl.ds(r0, QBLK), 0:D] = (open_k[0] * LN2).astype(BF16)
            gkv_ext[pl.ds(r0, QBLK), D:] = open_v[0].astype(BF16)
            open_k, open_v = open_k[1:], open_v[1:]
        for t in range(spans - 1):
            open_scr[0, t * QBLK : (t + 1) * QBLK, :] = open_k[t]
            open_scr[1, t * QBLK : (t + 1) * QBLK, :] = open_v[t]

    section("bwd", step, blocks // bwd_size, bwd_group)
    gkv_ext[rows:, 0:D] = (open_scr[0] * LN2).astype(BF16)
    gkv_ext[rows:, D:] = open_scr[1].astype(BF16)
    sendlow_ref[0] = dot_t(gkv_ext[0:RIM, :], wkv[...]).astype(BF16)
    sendhigh_ref[0] = dot_t(gkv_ext[RIM + rows :, :], wkv[...]).astype(BF16)
    gkv_ref[0] = gkv_ext[RIM : RIM + rows, :]
    grad_qg = t_dot(hid[RIM : RIM + rows, :], gqg_ref[0])
    grad_kv = t_dot(hid[...], gkv_ext[...])
    for at, part in ((0, grad_qg[:, 0:D]), (1, grad_kv[:, 0:D]), (2, grad_kv[:, D:]), (3, grad_qg[:, D:])):
        acc_ref[at * D : (at + 1) * D, :] += part

    @pl.when(step == pl.num_programs(0) - 1)
    def _():
        terms = jnp.zeros((D, D), F32)
        for at, w_ref in enumerate((wq_ref, wk_ref, wv_ref, wg_ref)):
            terms += acc_ref[at * D : (at + 1) * D, :] * w_ref[...].astype(F32)
        by_channel = jnp.broadcast_to(jnp.sum(terms, axis=1, keepdims=True), (D, D)).T
        acc_ref[TAIL_AT : TAIL_AT + 8, :] = jnp.where(
            iota((8, D), 0) == 0, by_channel[0:8] / gain, 0.0
        )
        sum_ref[...] = acc_ref[...].astype(BF16)


def main_call(counts, memb, atoms, low, high, cot, gain, wq, wk, wv, wg, wout, wtok, bias):
    samples, rows, _ = atoms.shape
    ext = rows + 2 * RIM
    width = wtok.shape[1]
    blocks = rows // QBLK
    hq = HEADS * QBLK

    def per_sample(*shape):
        return pl.BlockSpec((1,) + shape, lambda s: (s,) + (0,) * len(shape))

    def whole(*shape):
        return pl.BlockSpec(shape, lambda s: (0,) * len(shape))

    sd = jax.ShapeDtypeStruct
    return pl.pallas_call(
        main_kernel,
        grid=(samples,),
        out_shape=(
            sd((samples, TOK_DEV, width), BF16),
            sd((samples, rows, 2 * D), BF16),
            sd((samples, rows, 2 * D), BF16),
            sd((samples, rows, D), BF16),
            sd((samples, RIM, D), BF16),
            sd((samples, RIM, D), BF16),
            sd((ACC_ROWS, D), BF16),
            sd((blocks, hq, KWIN), F32),
        ),
        in_specs=[
            pl.BlockSpec(memory_space=pltpu.SMEM),
            whole(1, rows),
            per_sample(rows, D),
            per_sample(RIM, D),
            per_sample(RIM, D),
            per_sample(TOK_DEV, width),
            whole(1, D),
            whole(D, D),
            whole(D, D),
            whole(D, D),
            whole(D, D),
            whole(D, D),
            whole(D, width),
            whole(blocks, hq, KWIN),
        ],
        out_specs=(
            per_sample(TOK_DEV, width),
            per_sample(rows, 2 * D),
            per_sample(rows, 2 * D),
            per_sample(rows, D),
            per_sample(RIM, D),
            per_sample(RIM, D),
            whole(ACC_ROWS, D),
            whole(blocks, hq, KWIN),
        ),
        scratch_shapes=[
            pltpu.VMEM((D, 2 * D), BF16),
            pltpu.VMEM((D, 2 * D), BF16),
            pltpu.VMEM((width, D), BF16),
            pltpu.VMEM((D, D), BF16),
            pltpu.VMEM((TOK_DEV, rows), BF16),
            pltpu.VMEM((rows, 2 * TOK_DEV), BF16),
            pltpu.VMEM((TOK_DEV, D), F32),
            pltpu.VMEM((ext, D), BF16),
            pltpu.VMEM((ext, D), BF16),
            pltpu.VMEM((ext, 2 * D), BF16),
            pltpu.VMEM((rows, D), BF16),
            pltpu.VMEM((rows, D), F32),
            pltpu.VMEM((rows, D), F32),
            pltpu.VMEM((rows, D), F32),
            pltpu.VMEM((blocks, hq, D), BF16),
            pltpu.VMEM((blocks, hq, KWIN), BF16),
            pltpu.VMEM((rows, D), BF16),
            pltpu.VMEM((rows, width), BF16),
            pltpu.VMEM((rows, width), BF16),
            pltpu.VMEM((rows, D), BF16),
            pltpu.VMEM((rows, D), BF16),
            pltpu.VMEM((ext, 2 * D), BF16),
            pltpu.VMEM((2, 2 * RIM, D), F32),
            pltpu.VMEM((2 * TOK_DEV, width), BF16),
            pltpu.VMEM((ACC_ROWS, D), F32),
        ],
        compiler_params=pltpu.CompilerParams(
            vmem_limit_bytes=VMEM_LIMIT, dimension_semantics=("arbitrary",)
        ),
        name="atom_layer",
    )(counts, memb, atoms, low, high, cot, gain, wq, wk, wv, wg, wout, wtok, bias)


def finish_kernel(
    atoms_ref, gqg_ref, gkv_ref, gu_ref, left_ref, right_ref, gain_ref, wq_ref, wk_ref, wv_ref, wg_ref, *rest
):
    gatoms_ref = rest[-1]
    rows = atoms_ref.shape[1]
    gain = gain_ref[...]
    wqg = jnp.concatenate([wq_ref[...], wg_ref[...]], axis=1)
    wkv = jnp.concatenate([wk_ref[...], wv_ref[...]], axis=1)
    size = 128
    for c0 in range(0, rows, size):
        sl = slice(c0, c0 + size)
        gh = dot_t(gqg_ref[0, sl, :], wqg) + dot_t(gkv_ref[0, sl, :], wkv)
        if c0 == 0:
            gh = jnp.concatenate([gh[0:RIM] + left_ref[0].astype(F32), gh[RIM:]], axis=0)
        if c0 + size == rows:
            gh = jnp.concatenate(
                [gh[: size - RIM], gh[size - RIM :] + right_ref[0].astype(F32)], axis=0
            )
        normed, inv_std = layer_norm(atoms_ref[0, sl, :].astype(F32))
        ga = gu_ref[0, sl, :].astype(F32) + ln_backward(gh, gain, normed, inv_std)
        gatoms_ref[0, sl, :] = ga.astype(BF16)


def finish_call(first, number, atoms, gqg, gkv, gu, from_left, from_right, gain, ws, held):
    samples, rows, _ = atoms.shape

    def per_sample(*shape):
        return pl.BlockSpec((1,) + shape, lambda s: (s + first,) + (0,) * len(shape))

    def whole(*shape):
        return pl.BlockSpec(shape, lambda s: (0,) * len(shape))

    specs = [
        per_sample(rows, D),
        per_sample(rows, 2 * D),
        per_sample(rows, 2 * D),
        per_sample(rows, D),
        per_sample(RIM, D),
        per_sample(RIM, D),
        whole(1, D),
    ] + [whole(D, D)] * 4
    operands = [atoms, gqg, gkv, gu, from_left, from_right, gain, *ws]
    aliases = {}
    if held is not None:
        specs.append(pl.BlockSpec(memory_space=pl.ANY))
        aliases = {len(operands): 0}
        operands.append(held)
    return pl.pallas_call(
        finish_kernel,
        grid=(number,),
        out_shape=jax.ShapeDtypeStruct(atoms.shape, BF16),
        in_specs=specs,
        out_specs=per_sample(rows, D),
        input_output_aliases=aliases,
        compiler_params=pltpu.CompilerParams(dimension_semantics=("arbitrary",)),
        cost_estimate=pl.CostEstimate(
            flops=number * rows * D * 4 * D * 2,
            bytes_accessed=number * rows * D * 14,
            transcendentals=0,
        ),
        name="finish",
    )(*operands)


def route(count, digits, k):
    out = []
    total = 1
    for _, size in digits:
        total *= size
    for i in range(count):
        c, m = 0, 1
        for stride, size in digits:
            c += (i // stride % size) * m
            m *= size
        q = (c + k) % total
        j = i
        for stride, size in digits:
            j += (q % size - i // stride % size) * stride
            q //= size
        out.append((i, j))
    return out


def group_size(digits):
    total = 1
    for _, size in digits:
        total *= size
    return total


def exchange_sum(x, axis, digits):
    count = lax.axis_size(axis)
    low = x.astype(BF16)
    total = low.astype(F32)
    for k in range(1, group_size(digits)):
        total = total + lax.ppermute(low, axis, route(count, digits, k)).astype(F32)
    return total


def scatter_sum(x, axis):
    count = lax.axis_size(axis)
    me = lax.axis_index(axis)
    size = x.shape[0] // count
    low = x.astype(BF16)
    total = lax.dynamic_slice_in_dim(low, me * size, size, 0).astype(F32)
    for k in range(1, count):
        piece = lax.dynamic_slice_in_dim(low, (me + k) % count * size, size, 0)
        total = total + lax.ppermute(piece, axis, route(count, [(1, count)], k)).astype(F32)
    return total


def gather(x, axis):
    count = lax.axis_size(axis)
    me = lax.axis_index(axis)
    size = x.shape[0]
    low = x.astype(BF16)
    out = jnp.zeros((count * size,) + x.shape[1:], BF16)
    out = lax.dynamic_update_slice_in_dim(out, low, me * size, 0)
    for k in range(1, count):
        piece = lax.ppermute(low, axis, route(count, [(1, count)], k))
        out = lax.dynamic_update_slice_in_dim(out, piece, (me - k) % count * size, 0)
    return out


def seq_stages(count):
    stages, stride = [], 1
    for size in RADIX:
        size = min(size, count // stride)
        if size > 1:
            stages.append([(stride, size)])
        stride *= size
    return stages


def shifted(block, axis, distance):
    devices = range(lax.axis_size(axis))
    moves = [(i - distance, i) for i in devices if i - distance in devices]
    return lax.ppermute(block, axis, moves)


def sums_and_finish(
    acc, score_sum, pair, atoms, gqg, gkv, gu, send_low, send_high, gain_row, ws, width
):
    samples = atoms.shape[0]
    total = scatter_sum(acc, "samp")
    from_right = shifted(send_low, "seq", -1)
    from_left = shifted(send_high, "seq", 1)
    pair_part = pair_grad_call(pair, score_sum)
    pair_sum = jnp.sum(pair_part[:HEADS].reshape(HEADS, KWIN, CP), axis=1).reshape(1, HEADS * CP)
    pair_rows = jnp.pad(pair_sum, ((0, 15), (0, D - HEADS * CP)))
    main_rows = total.shape[0]
    total = jnp.concatenate([total, pair_rows], axis=0)
    stages = seq_stages(lax.axis_size("seq"))
    share = samples // FINISH_PIECES
    begin = max(len(stages) - FINISH_PIECES + FINISH_LATE, 0)
    grad_atoms, piece = None, 0
    for at, digits in enumerate(stages):
        if at == begin:
            total, from_left, from_right = lax.optimization_barrier((total, from_left, from_right))
        if at >= begin and piece < FINISH_PIECES - FINISH_LATE:
            grad_atoms = finish_call(
                piece * share, share, atoms, gqg, gkv, gu, from_left, from_right, gain_row, ws, grad_atoms
            )
            piece += 1
        total = exchange_sum(total, "seq", digits)
        if grad_atoms is not None:
            total, grad_atoms = lax.optimization_barrier((total, grad_atoms))
    for last in range(piece, FINISH_PIECES):
        grad_atoms = finish_call(
            last * share, share, atoms, gqg, gkv, gu, from_left, from_right, gain_row, ws, grad_atoms
        )
    parts = gather(total, "samp").astype(F32).reshape(-1, main_rows + 16, D)
    tail = jnp.sum(parts[:, main_rows:], axis=0)
    flat = parts[:, :main_rows].reshape(-1, D)
    mats = [flat[i * D : (i + 1) * D] for i in range(5 + width // D)]
    gain_total = flat[TAIL_AT]
    grad_pair = tail[0, : HEADS * CP].reshape(HEADS, CP).T
    return grad_atoms, gain_total, mats, grad_pair


def on_device(
    atoms,
    gain,
    w_query,
    w_key,
    w_value,
    w_gate,
    w_out,
    w_token,
    w_pair,
    pair_cond,
    counts,
    membership,
    pooled_cot,
):
    samples, rows, _ = atoms.shape
    low = shifted(atoms[:, rows - RIM :], "seq", 1)
    high = shifted(atoms[:, :RIM], "seq", -1)
    pair = pair_cond.reshape(rows, KWIN * CP)
    bias = pair_bias_call(counts, pair, w_pair)
    gain_row = gain.reshape(1, D)
    ws = (w_query, w_key, w_value, w_gate)
    pooled, gqg, gkv, gu, send_low, send_high, acc, score_sum = main_call(
        counts,
        membership.reshape(1, rows),
        atoms,
        low,
        high,
        pooled_cot,
        gain_row,
        *ws,
        w_out,
        w_token,
        bias,
    )
    grad_atoms, gain_total, mats, grad_pair = sums_and_finish(
        acc, score_sum, pair, atoms, gqg, gkv, gu, send_low, send_high, gain_row, ws, w_token.shape[1]
    )
    return (
        pooled,
        grad_atoms,
        gain_total,
        mats[0],
        mats[1],
        mats[2],
        mats[3],
        mats[4],
        jnp.concatenate(mats[5:], axis=1),
        grad_pair,
    )


def solution(mesh):
    placed = (
        P("samp", "seq", None),
        P(),
        P(),
        P(),
        P(),
        P(),
        P(),
        P(),
        P(),
        P("seq", None, None),
        P(),
        P("seq"),
        P("samp", "seq", None),
    )
    return jax.shard_map(
        on_device,
        mesh=mesh,
        in_specs=placed,
        out_specs=(
            P("samp", "seq", None),
            P("samp", "seq", None),
            P(),
            P(),
            P(),
            P(),
            P(),
            P(),
            P(),
            P(),
        ),
        check_vma=False,
    )
```

```python
import jax
import jax.numpy as jnp
from jax import lax
from jax.experimental import pallas as pl
from jax.experimental.pallas import tpu as pltpu
from jax.sharding import PartitionSpec as P

HEADS = 4
QBLK = 32
KWIN = 128
TOK_DEV = 48
RIM = (KWIN - QBLK) // 2
D = 128
CP = 16

epsilon = 1e-05
LOG2E = 1.4426950408889634
LN2 = 0.6931471805599453
SCALING = 32.0 ** -0.5
F32 = jnp.float32
BF16 = jnp.bfloat16
OUT_AT = 4
TAIL_AT = 11 * D
ACC_ROWS = TAIL_AT + 64
GROUP = 4
PLAN = {"ln": "line", "fwd": "line", "tok": "line", "post": "line", "pool": "line", "bwd": "block"}
RADIX = (4, 4, 4)
FINISH_PIECES = 3
FINISH_LATE = 1
VMEM_LIMIT = 56 * 1024 * 1024


def dot(a, b):
    return lax.dot_general(a, b, (((1,), (0,)), ((), ())), preferred_element_type=F32)


def dot_t(a, b):
    return lax.dot_general(a, b, (((1,), (1,)), ((), ())), preferred_element_type=F32)


def t_dot(a, b):
    return lax.dot_general(a, b, (((0,), (0,)), ((), ())), preferred_element_type=F32)


def iota(shape, dim):
    return lax.broadcasted_iota(jnp.int32, shape, dim)


def live_counts(counts_ref):
    shard = lax.axis_index("seq")
    last = counts_ref.shape[0] - 1
    left = jnp.where(shard > 0, counts_ref[jnp.maximum(shard - 1, 0)], 0)
    right = jnp.where(shard < last, counts_ref[jnp.minimum(shard + 1, last)], 0)
    return left, counts_ref[shard], right


def bias_kernel(counts_ref, pair_ref, wpair_ref, bias_ref, w_scr):
    rows = pair_ref.shape[0]
    span = w_scr.shape[1]
    key_of_row = iota((KWIN, CP, span), 0)
    key_of_lane = iota((KWIN, CP, span), 2) % KWIN
    w_pair = wpair_ref[...].astype(F32)
    wcol = jnp.concatenate(
        [jnp.broadcast_to(w_pair[:, h : h + 1], (CP, KWIN)) for h in range(HEADS)], axis=1
    )
    wide = jnp.broadcast_to(wcol[None], (KWIN, CP, span))
    w_scr[...] = (
        jnp.where(key_of_row == key_of_lane, wide, 0.0).astype(BF16).reshape(KWIN * CP, span)
    )
    left, own, right = live_counts(counts_ref)
    step = 128
    for r0 in range(0, rows, step):
        out = dot(pair_ref[r0 : r0 + step, :], w_scr[...])
        for q0 in range(0, step, QBLK):
            b = (r0 + q0) // QBLK
            slot = iota((1, KWIN), 1) + (b * QBLK - RIM)
            before, after = slot < 0, slot >= rows
            limit = jnp.where(before, left, jnp.where(after, right, own))
            place = jnp.where(before, slot + rows, jnp.where(after, slot - rows, slot))
            shift = jnp.where(place < limit, 0.0, -jnp.inf)
            for h in range(HEADS):
                bias_ref[b, h * QBLK : (h + 1) * QBLK, :] = (
                    out[q0 : q0 + QBLK, h * KWIN : (h + 1) * KWIN] * LOG2E + shift
                )


def pair_bias_call(counts, pair, w_pair):
    blocks = pair.shape[0] // QBLK
    return pl.pallas_call(
        bias_kernel,
        out_shape=jax.ShapeDtypeStruct((blocks, HEADS * QBLK, KWIN), F32),
        in_specs=[
            pl.BlockSpec(memory_space=pltpu.SMEM),
            pl.BlockSpec(memory_space=pltpu.VMEM),
            pl.BlockSpec(memory_space=pltpu.VMEM),
        ],
        out_specs=pl.BlockSpec(memory_space=pltpu.VMEM),
        scratch_shapes=[pltpu.VMEM((KWIN * CP, HEADS * KWIN), BF16)],
        compiler_params=pltpu.CompilerParams(vmem_limit_bytes=VMEM_LIMIT),
        cost_estimate=pl.CostEstimate(
            flops=2 * pair.shape[0] * KWIN * CP * HEADS * KWIN,
            bytes_accessed=5 << 20,
            transcendentals=0,
        ),
        name="pair_bias",
    )(counts, pair, w_pair)


def pair_grad_kernel(pair_ref, score_ref, out_ref, g_scr):
    blocks = score_ref.shape[0]
    wide = KWIN * CP
    key_of_lane = iota((KWIN, wide), 1) // CP
    own_key = key_of_lane == iota((KWIN, wide), 0)
    rows = []
    for h in range(HEADS):
        for b in range(blocks):
            g_scr[b * QBLK : (b + 1) * QBLK, :] = score_ref[
                b, h * QBLK : (h + 1) * QBLK, :
            ].astype(BF16)
        prod = t_dot(g_scr[...], pair_ref[...])
        rows.append(jnp.sum(jnp.where(own_key, prod, 0.0), axis=0, keepdims=True))
    stacked = jnp.concatenate(rows + [jnp.zeros((8 - HEADS, wide), F32)], axis=0)
    out_ref[...] = stacked


def pair_grad_call(pair, score_sum):
    return pl.pallas_call(
        pair_grad_kernel,
        out_shape=jax.ShapeDtypeStruct((8, KWIN * CP), F32),
        in_specs=[pl.BlockSpec(memory_space=pltpu.VMEM)] * 2,
        out_specs=pl.BlockSpec(memory_space=pltpu.VMEM),
        scratch_shapes=[pltpu.VMEM((pair.shape[0], KWIN), BF16)],
        compiler_params=pltpu.CompilerParams(vmem_limit_bytes=VMEM_LIMIT),
        cost_estimate=pl.CostEstimate(
            flops=2 * pair.shape[0] * KWIN * CP * HEADS * KWIN,
            bytes_accessed=3 << 20,
            transcendentals=0,
        ),
        name="pair_grad",
    )(pair, score_sum)


def layer_norm(x):
    mean = jnp.mean(x, axis=-1, keepdims=True)
    centred = x - mean
    variance = jnp.mean(centred * centred, axis=-1, keepdims=True)
    inv_std = lax.rsqrt(variance + epsilon)
    return centred * inv_std, inv_std


def ln_backward(gh, gain, normed, inv_std):
    gn = gh * gain
    return inv_std * (
        gn
        - jnp.mean(gn, axis=-1, keepdims=True)
        - normed * jnp.mean(gn * normed, axis=-1, keepdims=True)
    )


def pick_heads(o):
    head = iota((QBLK, D), 1) // (D // HEADS)
    r = o[0:QBLK]
    for h in range(1, HEADS):
        r = jnp.where(head == h, o[h * QBLK : (h + 1) * QBLK], r)
    return r


def aligned(x, n):
    return x if isinstance(x, int) else pl.multiple_of(x, n)


def section(name, step, count, body):
    def unrolled():
        for i in range(count):
            body(i)

    if PLAN[name] == "loop":
        pl.loop(0, count)(body)
    elif PLAN[name] == "block":
        pl.when(step >= 0)(unrolled)
    else:
        unrolled()


def main_kernel(
    counts_ref,
    memb_ref,
    atoms_ref,
    low_ref,
    high_ref,
    cot_ref,
    gain_ref,
    wq_ref,
    wk_ref,
    wv_ref,
    wg_ref,
    wout_ref,
    wtok_ref,
    bias_ref,
    pooled_ref,
    gqg_ref,
    gkv_ref,
    gu_ref,
    sendlow_ref,
    sendhigh_ref,
    sum_ref,
    score_ref,
    wqg,
    wkv,
    wtok_t,
    wout_t,
    mem_t,
    mem2,
    inv_scr,
    hid,
    k_ext,
    v1,
    q_scr,
    sig_scr,
    att_scr,
    rden_scr,
    q4_scr,
    e_scr,
    upd_scr,
    act_scr,
    gpre_scr,
    g_scr,
    nga_scr,
    gkv_ext,
    open_scr,
    cot2,
    acc_ref,
):
    rows = atoms_ref.shape[1]
    ext = rows + 2 * RIM
    blocks = rows // QBLK
    step = pl.program_id(0)
    mask4 = (
        (iota((HEADS * QBLK, D), 0) // QBLK == iota((HEADS * QBLK, D), 1) // (D // HEADS))
        .astype(F32)
        .astype(BF16)
    )

    @pl.when(step == 0)
    def _():
        acc_ref[...] = jnp.zeros_like(acc_ref)
        wqg[:, 0:D] = wq_ref[...]
        wtok_t[...] = wtok_ref[...].astype(F32).T.astype(BF16)
        wout_t[...] = wout_ref[...].astype(F32).T.astype(BF16)
        wqg[:, D:] = wg_ref[...]
        wkv[:, 0:D] = wk_ref[...]
        wkv[:, D:] = wv_ref[...]
        score_ref[...] = jnp.zeros_like(score_ref)
        v1[:, D:] = jnp.ones((ext, D), BF16)
        shard = lax.axis_index("seq")
        own, first = counts_ref[shard], shard * TOK_DEV
        local = memb_ref[...] - first
        slot = iota((D, rows), 1)
        hit = (local == iota((D, rows), 0)) & (slot < own)
        hit_f = jnp.where(hit, 1.0, 0.0)
        total = jnp.sum(hit_f, axis=1, keepdims=True)
        inv = 1.0 / jnp.maximum(total, 1.0)
        mem_t[...] = hit_f[0:TOK_DEV].astype(BF16)
        inv_scr[...] = jnp.broadcast_to(inv[0:TOK_DEV], inv_scr.shape)
        weighted = hit_f * inv
        high = weighted.astype(BF16)
        rest = (weighted - high.astype(F32)).astype(BF16)
        mem2[:, 0:TOK_DEV] = high.astype(F32).T.astype(BF16)[:, 0:TOK_DEV]
        mem2[:, TOK_DEV : 2 * TOK_DEV] = rest.astype(F32).T.astype(BF16)[:, 0:TOK_DEV]

    gain = gain_ref[...]
    fwd_size = blocks if PLAN["fwd"] != "loop" else GROUP
    bwd_size = blocks if PLAN["bwd"] != "loop" else GROUP
    def project(src, at, from_row, size):
        x = src[0, pl.ds(from_row, size), :].astype(F32)
        normed, _ = layer_norm(x)
        hidden = (normed * gain).astype(BF16)
        kv = dot(hidden, wkv[...]).astype(BF16)
        to = pl.ds(at, size)
        k_ext[to, :] = kv[:, 0:D]
        v1[to, 0:D] = kv[:, D:]
        hid[to, :] = hidden
        return hidden

    size = 128
    project(low_ref, 0, 0, RIM)
    project(high_ref, RIM + rows, 0, RIM)

    def ln_rows(c):
        c0 = aligned(c * size, size)
        hidden = project(atoms_ref, aligned(c0 + RIM, 16), c0, size)
        qg = dot(hidden, wqg[...])
        q_scr[pl.ds(c0, size), :] = (qg[:, 0:D] * (SCALING * LOG2E)).astype(BF16)
        sig_scr[pl.ds(c0, size), :] = 0.5 * jnp.tanh(0.5 * qg[:, D:]) + 0.5

    section("ln", step, rows // size, ln_rows)

    def fwd_group(g):
        for w in range(fwd_size):
            b = g * fwd_size + w
            r0 = aligned(b * QBLK, QBLK)
            q_b = q_scr[pl.ds(r0, QBLK), :]
            q4 = jnp.concatenate([q_b] * HEADS, axis=0) * mask4
            q4_scr[b] = q4
            scores = dot_t(q4, k_ext[pl.ds(r0, KWIN), :]) + bias_ref[b]
            e = jnp.exp2(scores).astype(BF16)
            e_scr[b] = e
            o = dot(e, v1[pl.ds(r0, KWIN), :])
            num = pick_heads(o[:, 0:D])
            rden = 1.0 / pick_heads(o[:, D:])
            att_scr[pl.ds(r0, QBLK), :] = num * rden
            rden_scr[pl.ds(r0, QBLK), :] = rden

    section("fwd", step, blocks // fwd_size, fwd_group)

    cot2[0:TOK_DEV, :] = cot_ref[0]
    cot2[TOK_DEV:, :] = cot_ref[0]
    cols = 256
    width = wtok_ref.shape[1]

    def tok_rows(c):
        sl = pl.ds(aligned(c * 256, 256), 256)
        gated = (sig_scr[sl, :] * att_scr[sl, :]).astype(BF16)
        upd = (atoms_ref[0, sl, :].astype(F32) + dot(gated, wout_ref[...])).astype(BF16)
        upd_scr[sl, :] = upd
        for t0 in range(0, width, cols):
            cs = slice(t0, t0 + cols)
            pre = dot(upd, wtok_ref[:, cs])
            sg = 0.5 * jnp.tanh(0.5 * pre) + 0.5
            act = pre * sg
            act_scr[sl, cs] = act.astype(BF16)
            grad_act = dot(mem2[sl, :], cot2[:, cs])
            gpre_scr[sl, cs] = (grad_act * (sg + act * (1.0 - sg))).astype(BF16)

    section("tok", step, rows // 256, tok_rows)

    def post_rows(c):
        sl = pl.ds(aligned(c * 256, 256), 256)
        gu = dot(gpre_scr[sl, :], wtok_t[...]).astype(BF16)
        gu_ref[0, sl, :] = gu
        sig = sig_scr[sl, :]
        att = att_scr[sl, :]
        gated = (sig * att).astype(BF16)
        acc_ref[OUT_AT * D : (OUT_AT + 1) * D, :] += t_dot(gated, gu)
        gatt = dot(gu, wout_t[...]) * sig
        gatt_att = gatt * att
        gqg_ref[0, sl, D:] = (gatt_att * (1.0 - sig)).astype(BF16)
        rden = rden_scr[sl, :]
        g_scr[sl, :] = (gatt * rden).astype(BF16)
        nga_scr[sl, :] = (-(gatt_att * rden)).astype(BF16)

    section("post", step, rows // 256, post_rows)

    def pool_cols(c):
        t0 = c * cols
        cs = slice(t0, t0 + cols)
        pooled_ref[0, :, cs] = (
            dot(mem_t[...], act_scr[:, cs]) * jnp.concatenate([inv_scr[...]] * (cols // D), axis=1)
        ).astype(BF16)
        grad_tok = t_dot(upd_scr[...], gpre_scr[:, cs])
        for t1 in range(0, cols, D):
            at = (OUT_AT + 1) * D + t0 + t1
            acc_ref[at : at + D, :] += grad_tok[:, t1 : t1 + D]

    section("pool", step, width // cols, pool_cols)

    spans = KWIN // QBLK
    open_scr[...] = jnp.zeros_like(open_scr)

    def bwd_group(g):
        open_k = [open_scr[0, t * QBLK : (t + 1) * QBLK, :] for t in range(spans - 1)]
        open_v = [open_scr[1, t * QBLK : (t + 1) * QBLK, :] for t in range(spans - 1)]
        for w in range(bwd_size):
            b = g * bwd_size + w
            r0 = aligned(b * QBLK, QBLK)
            g4 = jnp.concatenate([g_scr[pl.ds(r0, QBLK), :]] * HEADS, axis=0) * mask4
            nga4 = jnp.concatenate([nga_scr[pl.ds(r0, QBLK), :]] * HEADS, axis=0) * mask4
            e = e_scr[b]
            dp = dot_t(jnp.concatenate([g4, nga4], axis=1), v1[pl.ds(r0, KWIN), :])
            ds = e.astype(F32) * dp
            score_ref[b] += ds
            dsl = ds.astype(BF16)
            gq = pick_heads(dot(dsl, k_ext[pl.ds(r0, KWIN), :]))
            gqg_ref[0, pl.ds(r0, QBLK), 0:D] = (gq * SCALING).astype(BF16)
            gk = t_dot(dsl, q4_scr[b])
            gv = t_dot(e, g4)
            part_k = [gk[t * QBLK : (t + 1) * QBLK] for t in range(spans)]
            part_v = [gv[t * QBLK : (t + 1) * QBLK] for t in range(spans)]
            open_k = [x + y for x, y in zip(open_k, part_k)] + part_k[len(open_k) :]
            open_v = [x + y for x, y in zip(open_v, part_v)] + part_v[len(open_v) :]
            gkv_ext[pl.ds(r0, QBLK), 0:D] = (open_k[0] * LN2).astype(BF16)
            gkv_ext[pl.ds(r0, QBLK), D:] = open_v[0].astype(BF16)
            open_k, open_v = open_k[1:], open_v[1:]
        for t in range(spans - 1):
            open_scr[0, t * QBLK : (t + 1) * QBLK, :] = open_k[t]
            open_scr[1, t * QBLK : (t + 1) * QBLK, :] = open_v[t]

    section("bwd", step, blocks // bwd_size, bwd_group)
    gkv_ext[rows:, 0:D] = (open_scr[0] * LN2).astype(BF16)
    gkv_ext[rows:, D:] = open_scr[1].astype(BF16)
    sendlow_ref[0] = dot_t(gkv_ext[0:RIM, :], wkv[...]).astype(BF16)
    sendhigh_ref[0] = dot_t(gkv_ext[RIM + rows :, :], wkv[...]).astype(BF16)
    gkv_ref[0] = gkv_ext[RIM : RIM + rows, :]
    grad_qg = t_dot(hid[RIM : RIM + rows, :], gqg_ref[0])
    grad_kv = t_dot(hid[...], gkv_ext[...])
    for at, part in ((0, grad_qg[:, 0:D]), (1, grad_kv[:, 0:D]), (2, grad_kv[:, D:]), (3, grad_qg[:, D:])):
        acc_ref[at * D : (at + 1) * D, :] += part

    @pl.when(step == pl.num_programs(0) - 1)
    def _():
        terms = jnp.zeros((D, D), F32)
        for at, w_ref in enumerate((wq_ref, wk_ref, wv_ref, wg_ref)):
            terms += acc_ref[at * D : (at + 1) * D, :] * w_ref[...].astype(F32)
        by_channel = jnp.broadcast_to(jnp.sum(terms, axis=1, keepdims=True), (D, D)).T
        acc_ref[TAIL_AT : TAIL_AT + 8, :] = jnp.where(
            iota((8, D), 0) == 0, by_channel[0:8] / gain, 0.0
        )
        sum_ref[...] = acc_ref[...].astype(BF16)


def main_call(counts, memb, atoms, low, high, cot, gain, wq, wk, wv, wg, wout, wtok, bias):
    samples, rows, _ = atoms.shape
    ext = rows + 2 * RIM
    width = wtok.shape[1]
    blocks = rows // QBLK
    hq = HEADS * QBLK

    def per_sample(*shape):
        return pl.BlockSpec((1,) + shape, lambda s: (s,) + (0,) * len(shape))

    def whole(*shape):
        return pl.BlockSpec(shape, lambda s: (0,) * len(shape))

    sd = jax.ShapeDtypeStruct
    return pl.pallas_call(
        main_kernel,
        grid=(samples,),
        out_shape=(
            sd((samples, TOK_DEV, width), BF16),
            sd((samples, rows, 2 * D), BF16),
            sd((samples, rows, 2 * D), BF16),
            sd((samples, rows, D), BF16),
            sd((samples, RIM, D), BF16),
            sd((samples, RIM, D), BF16),
            sd((ACC_ROWS, D), BF16),
            sd((blocks, hq, KWIN), F32),
        ),
        in_specs=[
            pl.BlockSpec(memory_space=pltpu.SMEM),
            whole(1, rows),
            per_sample(rows, D),
            per_sample(RIM, D),
            per_sample(RIM, D),
            per_sample(TOK_DEV, width),
            whole(1, D),
            whole(D, D),
            whole(D, D),
            whole(D, D),
            whole(D, D),
            whole(D, D),
            whole(D, width),
            whole(blocks, hq, KWIN),
        ],
        out_specs=(
            per_sample(TOK_DEV, width),
            per_sample(rows, 2 * D),
            per_sample(rows, 2 * D),
            per_sample(rows, D),
            per_sample(RIM, D),
            per_sample(RIM, D),
            whole(ACC_ROWS, D),
            whole(blocks, hq, KWIN),
        ),
        scratch_shapes=[
            pltpu.VMEM((D, 2 * D), BF16),
            pltpu.VMEM((D, 2 * D), BF16),
            pltpu.VMEM((width, D), BF16),
            pltpu.VMEM((D, D), BF16),
            pltpu.VMEM((TOK_DEV, rows), BF16),
            pltpu.VMEM((rows, 2 * TOK_DEV), BF16),
            pltpu.VMEM((TOK_DEV, D), F32),
            pltpu.VMEM((ext, D), BF16),
            pltpu.VMEM((ext, D), BF16),
            pltpu.VMEM((ext, 2 * D), BF16),
            pltpu.VMEM((rows, D), BF16),
            pltpu.VMEM((rows, D), F32),
            pltpu.VMEM((rows, D), F32),
            pltpu.VMEM((rows, D), F32),
            pltpu.VMEM((blocks, hq, D), BF16),
            pltpu.VMEM((blocks, hq, KWIN), BF16),
            pltpu.VMEM((rows, D), BF16),
            pltpu.VMEM((rows, width), BF16),
            pltpu.VMEM((rows, width), BF16),
            pltpu.VMEM((rows, D), BF16),
            pltpu.VMEM((rows, D), BF16),
            pltpu.VMEM((ext, 2 * D), BF16),
            pltpu.VMEM((2, 2 * RIM, D), F32),
            pltpu.VMEM((2 * TOK_DEV, width), BF16),
            pltpu.VMEM((ACC_ROWS, D), F32),
        ],
        compiler_params=pltpu.CompilerParams(
            vmem_limit_bytes=VMEM_LIMIT, dimension_semantics=("arbitrary",)
        ),
        name="atom_layer",
    )(counts, memb, atoms, low, high, cot, gain, wq, wk, wv, wg, wout, wtok, bias)


def finish_kernel(
    atoms_ref, gqg_ref, gkv_ref, gu_ref, left_ref, right_ref, gain_ref, wq_ref, wk_ref, wv_ref, wg_ref, *rest
):
    gatoms_ref = rest[-1]
    rows = atoms_ref.shape[1]
    gain = gain_ref[...]
    wqg = jnp.concatenate([wq_ref[...], wg_ref[...]], axis=1)
    wkv = jnp.concatenate([wk_ref[...], wv_ref[...]], axis=1)
    size = 512
    for c0 in range(0, rows, size):
        sl = slice(c0, c0 + size)
        gh = dot_t(gqg_ref[0, sl, :], wqg) + dot_t(gkv_ref[0, sl, :], wkv)
        if c0 == 0:
            gh = jnp.concatenate([gh[0:RIM] + left_ref[0].astype(F32), gh[RIM:]], axis=0)
        if c0 + size == rows:
            gh = jnp.concatenate(
                [gh[: size - RIM], gh[size - RIM :] + right_ref[0].astype(F32)], axis=0
            )
        normed, inv_std = layer_norm(atoms_ref[0, sl, :].astype(F32))
        ga = gu_ref[0, sl, :].astype(F32) + ln_backward(gh, gain, normed, inv_std)
        gatoms_ref[0, sl, :] = ga.astype(BF16)


def finish_call(first, number, atoms, gqg, gkv, gu, from_left, from_right, gain, ws, held):
    samples, rows, _ = atoms.shape

    def per_sample(*shape):
        return pl.BlockSpec((1,) + shape, lambda s: (s + first,) + (0,) * len(shape))

    def whole(*shape):
        return pl.BlockSpec(shape, lambda s: (0,) * len(shape))

    specs = [
        per_sample(rows, D),
        per_sample(rows, 2 * D),
        per_sample(rows, 2 * D),
        per_sample(rows, D),
        per_sample(RIM, D),
        per_sample(RIM, D),
        whole(1, D),
    ] + [whole(D, D)] * 4
    operands = [atoms, gqg, gkv, gu, from_left, from_right, gain, *ws]
    aliases = {}
    if held is not None:
        specs.append(pl.BlockSpec(memory_space=pl.ANY))
        aliases = {len(operands): 0}
        operands.append(held)
    return pl.pallas_call(
        finish_kernel,
        grid=(number,),
        out_shape=jax.ShapeDtypeStruct(atoms.shape, BF16),
        in_specs=specs,
        out_specs=per_sample(rows, D),
        input_output_aliases=aliases,
        compiler_params=pltpu.CompilerParams(dimension_semantics=("arbitrary",)),
        cost_estimate=pl.CostEstimate(
            flops=number * rows * D * 4 * D * 2,
            bytes_accessed=number * rows * D * 14,
            transcendentals=0,
        ),
        name="finish",
    )(*operands)


def route(count, digits, k):
    out = []
    total = 1
    for _, size in digits:
        total *= size
    for i in range(count):
        c, m = 0, 1
        for stride, size in digits:
            c += (i // stride % size) * m
            m *= size
        q = (c + k) % total
        j = i
        for stride, size in digits:
            j += (q % size - i // stride % size) * stride
            q //= size
        out.append((i, j))
    return out


def group_size(digits):
    total = 1
    for _, size in digits:
        total *= size
    return total


def exchange_sum(x, axis, digits):
    count = lax.axis_size(axis)
    low = x.astype(BF16)
    total = low.astype(F32)
    for k in range(1, group_size(digits)):
        total = total + lax.ppermute(low, axis, route(count, digits, k)).astype(F32)
    return total


def scatter_sum(x, axis):
    count = lax.axis_size(axis)
    me = lax.axis_index(axis)
    size = x.shape[0] // count
    low = x.astype(BF16)
    total = lax.dynamic_slice_in_dim(low, me * size, size, 0).astype(F32)
    for k in range(1, count):
        piece = lax.dynamic_slice_in_dim(low, (me + k) % count * size, size, 0)
        total = total + lax.ppermute(piece, axis, route(count, [(1, count)], k)).astype(F32)
    return total


def gather(x, axis):
    count = lax.axis_size(axis)
    me = lax.axis_index(axis)
    size = x.shape[0]
    low = x.astype(BF16)
    out = jnp.zeros((count * size,) + x.shape[1:], BF16)
    out = lax.dynamic_update_slice_in_dim(out, low, me * size, 0)
    for k in range(1, count):
        piece = lax.ppermute(low, axis, route(count, [(1, count)], k))
        out = lax.dynamic_update_slice_in_dim(out, piece, (me - k) % count * size, 0)
    return out


def seq_stages(count):
    stages, stride = [], 1
    for size in RADIX:
        size = min(size, count // stride)
        if size > 1:
            stages.append([(stride, size)])
        stride *= size
    return stages[::-1]


def shifted(block, axis, distance):
    devices = range(lax.axis_size(axis))
    moves = [(i - distance, i) for i in devices if i - distance in devices]
    return lax.ppermute(block, axis, moves)


def sums_and_finish(
    acc, score_sum, pair, atoms, gqg, gkv, gu, send_low, send_high, gain_row, ws, width
):
    samples = atoms.shape[0]
    total = scatter_sum(acc, "samp")
    from_right = shifted(send_low, "seq", -1)
    from_left = shifted(send_high, "seq", 1)
    pair_part = pair_grad_call(pair, score_sum)
    pair_sum = jnp.sum(pair_part[:HEADS].reshape(HEADS, KWIN, CP), axis=1).reshape(1, HEADS * CP)
    pair_rows = jnp.pad(pair_sum, ((0, 15), (0, D - HEADS * CP)))
    main_rows = total.shape[0]
    total = jnp.concatenate([total, pair_rows], axis=0)
    stages = seq_stages(lax.axis_size("seq"))
    share = samples // FINISH_PIECES
    begin = max(len(stages) - FINISH_PIECES + FINISH_LATE, 0)
    grad_atoms, piece = None, 0
    for at, digits in enumerate(stages):
        if at == begin:
            total, from_left, from_right = lax.optimization_barrier((total, from_left, from_right))
        if at >= begin and piece < FINISH_PIECES - FINISH_LATE:
            grad_atoms = finish_call(
                piece * share, share, atoms, gqg, gkv, gu, from_left, from_right, gain_row, ws, grad_atoms
            )
            piece += 1
        total = exchange_sum(total, "seq", digits)
        if grad_atoms is not None:
            total, grad_atoms = lax.optimization_barrier((total, grad_atoms))
    for last in range(piece, FINISH_PIECES):
        grad_atoms = finish_call(
            last * share, share, atoms, gqg, gkv, gu, from_left, from_right, gain_row, ws, grad_atoms
        )
    parts = gather(total, "samp").astype(F32).reshape(-1, main_rows + 16, D)
    tail = jnp.sum(parts[:, main_rows:], axis=0)
    flat = parts[:, :main_rows].reshape(-1, D)
    mats = [flat[i * D : (i + 1) * D] for i in range(5 + width // D)]
    gain_total = flat[TAIL_AT]
    grad_pair = tail[0, : HEADS * CP].reshape(HEADS, CP).T
    return grad_atoms, gain_total, mats, grad_pair


def on_device(
    atoms,
    gain,
    w_query,
    w_key,
    w_value,
    w_gate,
    w_out,
    w_token,
    w_pair,
    pair_cond,
    counts,
    membership,
    pooled_cot,
):
    samples, rows, _ = atoms.shape
    low = shifted(atoms[:, rows - RIM :], "seq", 1)
    high = shifted(atoms[:, :RIM], "seq", -1)
    pair = pair_cond.reshape(rows, KWIN * CP)
    bias = pair_bias_call(counts, pair, w_pair)
    gain_row = gain.reshape(1, D)
    ws = (w_query, w_key, w_value, w_gate)
    pooled, gqg, gkv, gu, send_low, send_high, acc, score_sum = main_call(
        counts,
        membership.reshape(1, rows),
        atoms,
        low,
        high,
        pooled_cot,
        gain_row,
        *ws,
        w_out,
        w_token,
        bias,
    )
    grad_atoms, gain_total, mats, grad_pair = sums_and_finish(
        acc, score_sum, pair, atoms, gqg, gkv, gu, send_low, send_high, gain_row, ws, w_token.shape[1]
    )
    return (
        pooled,
        grad_atoms,
        gain_total,
        mats[0],
        mats[1],
        mats[2],
        mats[3],
        mats[4],
        jnp.concatenate(mats[5:], axis=1),
        grad_pair,
    )


def solution(mesh):
    placed = (
        P("samp", "seq", None),
        P(),
        P(),
        P(),
        P(),
        P(),
        P(),
        P(),
        P(),
        P("seq", None, None),
        P(),
        P("seq"),
        P("samp", "seq", None),
    )
    return jax.shard_map(
        on_device,
        mesh=mesh,
        in_specs=placed,
        out_specs=(
            P("samp", "seq", None),
            P("samp", "seq", None),
            P(),
            P(),
            P(),
            P(),
            P(),
            P(),
            P(),
            P(),
        ),
        check_vma=False,
    )
```
